32 devices in a mesh: section: 2 (over core), fsdp: 4 (over z), tensor: 4 (over y, x).
Axes of the slice: x: 2, y: 2, z: 4, core: 2. Of those that a mesh axis runs over, the one named last changes fastest.
Arguments:
- inputs: bfloat16 [2, 4096, 640], P(None, ('fsdp', 'tensor')), may hold values from -6 to 6
- out_grad: bfloat16 [2, 4096, 640], P(None, ('fsdp', 'tensor')), may hold values from -6 to 6
- segment_ids: int32 [2, 4096], P(None, 'fsdp'), may hold values from 0 to 1, as said below
- positions: int32 [2, 4096], P(None, 'fsdp'), may hold values from 0 to 1023, as said below
- before_gain: bfloat16 [2, 640], P('section', 'fsdp'), may hold values from 0.25 to 1.75
- query_matrix: bfloat16 [2, 640, 1024], P('section', 'fsdp', 'tensor'), may hold values from -0.25 to 0.25
- key_matrix: bfloat16 [2, 640, 256], P('section', 'fsdp'), may hold values from -0.25 to 0.25
- value_matrix: bfloat16 [2, 640, 256], P('section', 'fsdp'), may hold values from -0.25 to 0.25
- query_gain: bfloat16 [2, 256], P('section', 'fsdp'), may hold values from 0.25 to 1.75
- key_gain: bfloat16 [2, 256], P('section', 'fsdp'), may hold values from 0.25 to 1.75
- output_matrix: bfloat16 [2, 1024, 640], P('section', 'tensor', 'fsdp'), may hold values from -0.1875 to 0.1875
- after_gain: bfloat16 [2, 640], P('section', 'fsdp'), may hold values from 0.25 to 1.75
- feed_gain: bfloat16 [2, 640], P('section', 'fsdp'), may hold values from 0.25 to 1.75
- gate_matrix: bfloat16 [2, 640, 2048], P('section', 'fsdp', 'tensor'), may hold values from -0.25 to 0.25
- up_matrix: bfloat16 [2, 640, 2048], P('section', 'fsdp', 'tensor'), may hold values from -0.25 to 0.25
- down_matrix: bfloat16 [2, 2048, 640], P('section', 'tensor', 'fsdp'), may hold values from -0.125 to 0.125
- final_gain: bfloat16 [2, 640], P('section', 'fsdp'), may hold values from 0.25 to 1.75
Outputs:
- layer_out: bfloat16 [2, 2, 4096, 640], P('section', None, ('fsdp', 'tensor'))
- input_grad: float32 [2, 2, 4096, 640], P('section', None, ('fsdp', 'tensor'))
- grad_before_gain: float32 [2, 640], P('section', 'fsdp')
- grad_query_matrix: float32 [2, 640, 1024], P('section', 'fsdp', 'tensor')
- grad_key_matrix: float32 [2, 640, 256], P('section', 'fsdp')
- grad_value_matrix: float32 [2, 640, 256], P('section', 'fsdp')
- grad_query_gain: float32 [2, 256], P('section', 'fsdp')
- grad_key_gain: float32 [2, 256], P('section', 'fsdp')
- grad_output_matrix: float32 [2, 1024, 640], P('section', 'tensor', 'fsdp')
- grad_after_gain: float32 [2, 640], P('section', 'fsdp')
- grad_feed_gain: float32 [2, 640], P('section', 'fsdp')
- grad_gate_matrix: float32 [2, 640, 2048], P('section', 'fsdp', 'tensor')
- grad_up_matrix: float32 [2, 640, 2048], P('section', 'fsdp', 'tensor')
- grad_down_matrix: float32 [2, 2048, 640], P('section', 'tensor', 'fsdp')
- grad_final_gain: float32 [2, 640], P('section', 'fsdp')
The draws below stay inside these ranges and needn't reach their ends.
Inputs may be any that keep to these rules, and one draw needn't show every extreme that they name: `segment_ids`: within each aligned block of 1024 tokens of a micro-batch (one data rank's pack) the ids never fall and hold one or two sequences; one of them has more than 768 tokens. Each sequence's positions count 0, 1, 2, ... from its first token.
All inputs are finite; a program needn't handle non-finite values.
Results may differ from the reference program's by a relative error of at most 0.03.
Values may be sent and summed in bfloat16 or wider, within the bound.
No kernel may reach another device: no remote copies, remote signals or barrier semaphores. Data moves between devices by JAX's collectives and lax.ppermute only.
A program may use at most 192 MiB of HBM per device.

```python
import jax
import jax.numpy as jnp
from jax import lax

D = 640
HEADS = 4
HD = 256
FF = 2048
WINDOW = 512
MICRO = 2
TOK_DEV = 256
GROUP = 1024
TOKENS = 4096
SECTIONS = 2


def pack_layout(key):
    pack_count = MICRO * (TOKENS // GROUP)
    key_rest, key_order, key_pick = jax.random.split(key, 3)
    remainder = jax.random.randint(key_rest, (pack_count,), 0, TOK_DEV)
    main_order = jax.random.randint(key_order, (pack_count,), 0, 2)
    picked = jax.random.randint(key_pick, (), 0, pack_count)
    pack_index = jnp.arange(pack_count)
    remainder = jnp.where(pack_index == picked, 0, remainder)
    remainder = jnp.where(pack_index == (picked + 1) % pack_count, TOK_DEV - 1, remainder)
    boundary = jnp.where(main_order == 1, GROUP - remainder, remainder)
    token_place = jnp.arange(GROUP)
    later_part = (token_place[None, :] >= boundary[:, None]).astype(jnp.int32)
    counted = token_place[None, :] - later_part * boundary[:, None]
    return (later_part.reshape(MICRO, TOKENS).astype(jnp.int32), counted.reshape(MICRO, TOKENS).astype(jnp.int32))


def draw_segment_ids(key, part):
    identity, counted = pack_layout(key)
    return identity


def draw_positions(key, part):
    identity, counted = pack_layout(key)
    return counted


def levels(own_key, dims, shards, low, high):
    loudness = 1.0
    for position, blocks in shards:
        draws = jax.random.uniform(jax.random.fold_in(jax.random.fold_in(own_key, 6), position), (blocks,), jnp.float32, low / len(shards), high / len(shards))
        loudness = loudness * jnp.repeat(jnp.exp(draws), dims[position] // blocks).reshape((-1,) + (1,) * (len(dims) - 1 - position))
    return loudness


def bell_draw(own_key, shape, scale, reach, pieces=(), kind=jnp.bfloat16):
    entries = scale * jax.random.normal(own_key, shape, jnp.float32)
    if pieces:
        entries = entries * levels(own_key, shape, pieces, -0.22, 0.18)
    return jnp.clip(entries, -reach, reach).astype(kind)


def setup_inputs(seed: int = 0) -> dict:
    key_of = jax.random.split(jax.random.key(seed), 18)
    return {
        "inputs": bell_draw(key_of[0], (MICRO, TOKENS, D), 1.0, 6.0, ((1, 16),)),
        "out_grad": bell_draw(key_of[1], (MICRO, TOKENS, D), 1.0, 6.0, ((1, 16),)),
        "segment_ids": draw_segment_ids(jax.random.fold_in(key_of[17], 71), 0),
        "positions": draw_positions(jax.random.fold_in(key_of[17], 71), 0),
        "before_gain": jnp.clip(1.0 + 0.15 * jax.random.normal(key_of[4], (SECTIONS, D), jnp.float32), 0.25, 1.75).astype(jnp.bfloat16),
        "query_matrix": bell_draw(key_of[5], (SECTIONS, D, HEADS * HD), D ** -0.5, 0.25, ((0, 2), (1, 4), (2, 4))),
        "key_matrix": bell_draw(key_of[6], (SECTIONS, D, HD), D ** -0.5, 0.25, ((0, 2), (1, 4))),
        "value_matrix": bell_draw(key_of[7], (SECTIONS, D, HD), D ** -0.5, 0.25, ((0, 2), (1, 4))),
        "query_gain": jnp.clip(1.0 + 0.15 * jax.random.normal(key_of[8], (SECTIONS, HD), jnp.float32), 0.25, 1.75).astype(jnp.bfloat16),
        "key_gain": jnp.clip(1.0 + 0.15 * jax.random.normal(key_of[9], (SECTIONS, HD), jnp.float32), 0.25, 1.75).astype(jnp.bfloat16),
        "output_matrix": bell_draw(key_of[10], (SECTIONS, HEADS * HD, D), (HEADS * HD) ** -0.5, 0.1875, ((0, 2), (1, 4), (2, 4))),
        "after_gain": jnp.clip(1.0 + 0.15 * jax.random.normal(key_of[11], (SECTIONS, D), jnp.float32), 0.25, 1.75).astype(jnp.bfloat16),
        "feed_gain": jnp.clip(1.0 + 0.15 * jax.random.normal(key_of[12], (SECTIONS, D), jnp.float32), 0.25, 1.75).astype(jnp.bfloat16),
        "gate_matrix": bell_draw(key_of[13], (SECTIONS, D, FF), D ** -0.5, 0.25, ((0, 2), (1, 4), (2, 4))),
        "up_matrix": bell_draw(key_of[14], (SECTIONS, D, FF), D ** -0.5, 0.25, ((0, 2), (1, 4), (2, 4))),
        "down_matrix": bell_draw(key_of[15], (SECTIONS, FF, D), FF ** -0.5, 0.125, ((0, 2), (1, 4), (2, 4))),
        "final_gain": jnp.clip(1.0 + 0.15 * jax.random.normal(key_of[16], (SECTIONS, D), jnp.float32), 0.25, 1.75).astype(jnp.bfloat16),
    }


@jax.custom_vjp
def low(v):
    return lax.optimization_barrier(v.astype(jnp.bfloat16)).astype(jnp.float32)

@jax.custom_vjp
def low_back(v):
    return v

def low_keep(v):
    return (low(v), None)

def low_pass(kept, grad):
    return (grad,)

def back_keep(v):
    return (v, None)

def back_low(kept, grad):
    return (low(grad),)
low.defvjp(low_keep, low_pass)
low_back.defvjp(back_keep, back_low)
EPSILON = 1e-06
TOP_PRECISION = lax.Precision.HIGHEST

def norm_rows(value_rows, gain_value):
    return value_rows * lax.rsqrt(lax.optimization_barrier(jnp.mean(value_rows * value_rows, axis=-1, keepdims=True)) + EPSILON) * gain_value

def angles(token_positions, head_width):
    half_depth = head_width // 2
    frequency = 10000.0 ** (-(jnp.arange(half_depth, dtype=jnp.float32) * 2.0) / head_width)
    return token_positions.astype(jnp.float32)[..., None] * frequency

def rotate(value_rows, turn_angle):
    half_depth = value_rows.shape[-1] // 2
    cosine = jnp.cos(turn_angle)
    sine_part = jnp.sin(turn_angle)
    first_half = value_rows[..., :half_depth]
    second = value_rows[..., half_depth:]
    return jnp.concatenate([first_half * cosine - second * sine_part, second * cosine + first_half * sine_part], axis=-1)

def key_block_rows(rows_in, fill_value):
    pad_rows = jnp.full((WINDOW,) + rows_in.shape[1:], fill_value, rows_in.dtype)
    padded = jnp.concatenate([pad_rows, rows_in]).reshape((-1, WINDOW) + rows_in.shape[1:])
    return jnp.concatenate([padded[:-1], padded[1:]], axis=1)

def window_mask(segments, token_positions):
    block_count = segments.shape[0] // WINDOW
    key_segments = key_block_rows(segments, -1)
    key_positions = key_block_rows(token_positions, 0)
    query_segments = segments.reshape(block_count, WINDOW)
    query_positions = token_positions.reshape(block_count, WINDOW)
    position_gap = query_positions[:, :, None] - key_positions[:, None, :]
    return (query_segments[:, :, None] == key_segments[:, None, :]) & (position_gap >= 0) & (position_gap < WINDOW)

def attend_pack(operands):
    queries, key_rows, value_rows, segments, token_positions = operands
    head_width = key_rows.shape[-1]
    block_count = segments.shape[0] // WINDOW
    query_block_rows = queries.reshape(block_count, WINDOW, queries.shape[1], head_width)
    key_tile = key_block_rows(key_rows, 0.0)
    value_tile = key_block_rows(value_rows, 0.0)
    logit_scores = jnp.einsum('jyre,jwe->jyrw', query_block_rows, key_tile, precision=TOP_PRECISION) * head_width ** (-0.5)
    logit_scores = low_back(logit_scores)
    allowed = window_mask(segments, token_positions)
    masked = jnp.where(allowed[:, :, None, :], logit_scores, -1e+30)
    largest = lax.optimization_barrier(jnp.max(masked, axis=-1, keepdims=True))
    exponent = jnp.exp(masked - largest)
    attention_weights = low(exponent / lax.optimization_barrier(jnp.sum(exponent, axis=-1, keepdims=True)))
    attended_values = jnp.einsum('ytfi,yij->ytfj', attention_weights, value_tile, precision=TOP_PRECISION)
    return attended_values.reshape(queries.shape)

def layer_forward(inputs_now, layer_params, segments, token_positions):
    before_gain, query_matrix, key_matrix, value_matrix, query_gain, key_gain, output_matrix, after_gain, feed_gain, gate_matrix, up_matrix, down_matrix, final_gain = layer_params
    pack_count = inputs_now.shape[0]
    group_rows = inputs_now.shape[1]
    head_width = key_matrix.shape[1]
    head_count = query_matrix.shape[1] // head_width
    normed = low(norm_rows(inputs_now, before_gain))
    query_raw = low_back(jnp.einsum('pgd,de->pge', normed, query_matrix, precision=TOP_PRECISION))
    key_raw = low_back(jnp.einsum('pgd,de->pge', normed, key_matrix, precision=TOP_PRECISION))
    value_rows = low_back(low(jnp.einsum('pgd,de->pge', normed, value_matrix, precision=TOP_PRECISION)))
    turn_angle = angles(token_positions, head_width)
    query_heads = query_raw.reshape(pack_count, group_rows, head_count, head_width)
    queries = low(rotate(norm_rows(query_heads, query_gain), turn_angle[:, :, None, :]))
    key_rows = low(rotate(norm_rows(key_raw, key_gain), turn_angle))
    attended_values = lax.map(jax.checkpoint(attend_pack), (queries, key_rows, value_rows, segments, token_positions))
    attended_values = low_back(low(attended_values)).reshape(pack_count, group_rows, head_count * head_width)
    attention_sum = low_back(jnp.einsum('pge,ed->pgd', attended_values, output_matrix, precision=TOP_PRECISION))
    hidden = inputs_now + norm_rows(attention_sum, after_gain)
    feed_in = low(norm_rows(hidden, feed_gain))
    gate_value = low_back(jnp.einsum('pgd,de->pge', feed_in, gate_matrix, precision=TOP_PRECISION))
    up_value = low_back(jnp.einsum('pgd,de->pge', feed_in, up_matrix, precision=TOP_PRECISION))
    product = low(jax.nn.gelu(gate_value, approximate=True) * up_value)
    branch = low_back(jnp.einsum('pge,ed->pgd', product, down_matrix, precision=TOP_PRECISION))
    return hidden + norm_rows(branch, final_gain)

def reference(inputs, out_grad, segment_ids, positions, before_gain, query_matrix, key_matrix, value_matrix, query_gain, key_gain, output_matrix, after_gain, feed_gain, gate_matrix, up_matrix, down_matrix, final_gain):
    micro_count = inputs.shape[0]
    token_count = inputs.shape[1]
    width = inputs.shape[2]
    pack_count = micro_count * (token_count // GROUP)
    segments = segment_ids.reshape(pack_count, GROUP)
    token_positions = positions.reshape(pack_count, GROUP)
    stored = (before_gain, query_matrix, key_matrix, value_matrix, query_gain, key_gain, output_matrix, after_gain, feed_gain, gate_matrix, up_matrix, down_matrix, final_gain)
    params = tuple((weight.astype(jnp.float32) for weight in stored))
    start_rows = inputs.astype(jnp.float32).reshape(pack_count, GROUP, width)
    probes = jnp.zeros((SECTIONS, pack_count, GROUP, width), jnp.float32)

    def whole_model(probe_rows, weight_set):
        current = start_rows
        layer_outs = []
        result = start_rows
        for layer_index in range(SECTIONS):
            if layer_index > 0:
                current = low_back(layer_outs[-1])
            layer_params = tuple((weight[layer_index] for weight in weight_set))
            result = layer_forward(current + probe_rows[layer_index], layer_params, segments, token_positions)
            layer_outs.append(low(result))
        return (result, jnp.stack(layer_outs))
    result, pullback, layer_outs = jax.vjp(whole_model, probes, params, has_aux=True)
    grad_probes, grad_params = pullback(out_grad.astype(jnp.float32).reshape(pack_count, GROUP, width))
    grad_before, grad_query, grad_key, grad_value, grad_qgain, grad_kgain, grad_output, grad_after, grad_feed, grad_gate, grad_up, grad_down, grad_final = grad_params
    shape_all = (SECTIONS, micro_count, token_count, width)
    return (layer_outs.astype(jnp.bfloat16).reshape(shape_all), grad_probes.reshape(shape_all), grad_before, grad_query, grad_key, grad_value, grad_qgain, grad_kgain, grad_output, grad_after, grad_feed, grad_gate, grad_up, grad_down, grad_final)
```

```python
import jax
import jax.numpy as jnp
from jax import lax
from jax.sharding import PartitionSpec as P

WINDOW = 512
EPSILON = 1e-06
LOW = jnp.bfloat16
WIDE = jnp.float32


def flip(value, axis, bit):
    count = lax.axis_size(axis)
    return lax.ppermute(value, axis, [(i, i ^ bit) for i in range(count)])


def ring(value, axis):
    count = lax.axis_size(axis)
    return lax.ppermute(value, axis, [(i, (i + 1) % count) for i in range(count)])


def shifted(value, axis, by):
    count = lax.axis_size(axis)
    pairs = [(i, i + by) for i in range(count) if 0 <= i + by < count]
    return lax.ppermute(value, axis, pairs)


def add(*parts):
    total = parts[0].astype(WIDE)
    for part in parts[1:]:
        total = total + part.astype(WIDE)
    return total


def dot(left, right):
    return jnp.dot(left, right, preferred_element_type=WIDE)


def dot_nt(left, right):
    return lax.dot_general(left, right, (((1,), (1,)), ((), ())), preferred_element_type=WIDE)


def dot_tn(left, right):
    return lax.dot_general(left, right, (((0,), (0,)), ((), ())), preferred_element_type=WIDE)


def gather_slabs(slab):
    ranks = lax.axis_size("fsdp")
    section = lax.axis_index("section")
    data = lax.axis_index("fsdp")
    head = lax.axis_index("tensor")
    rows, columns = slab.shape
    half = rows // 2
    current = slab
    if ranks > 4:
        current = lax.all_gather(slab, "fsdp", axis=0, tiled=True)
        data, ranks, rows, half = 0, 1, rows * ranks, rows * ranks // 2
    whole = jnp.zeros((2, 4, ranks, rows, columns), slab.dtype)
    for step in range(ranks):
        chunk = current
        place = (data - step) % ranks
        if step < ranks - 1:
            current = ring(current, "fsdp")
        near = flip(chunk, "tensor", 1)
        far = flip(chunk, "tensor", 2)
        across = jnp.concatenate([flip(far[:half], "tensor", 1), flip(near[half:], "tensor", 2)])
        for piece, bit in ((chunk, 0), (near, 1), (far, 2), (across, 3)):
            other = flip(piece, "section", 1)
            whole = lax.dynamic_update_slice(
                whole, piece[None, None, None], (section, head ^ bit, place, 0, 0)
            )
            whole = lax.dynamic_update_slice(
                whole, other[None, None, None], (1 - section, head ^ bit, place, 0, 0)
            )
    return whole


def scatter_slabs(whole):
    ranks = lax.axis_size("fsdp")
    section = lax.axis_index("section")
    data = lax.axis_index("fsdp")
    head = lax.axis_index("tensor")
    rows, columns = whole.shape[3:]
    spread = ranks > 4
    if spread:
        data, ranks, rows = 0, 1, rows * ranks
        whole = whole.reshape(2, 4, 1, rows, columns)
    half = rows // 2
    arriving = None
    total = None
    for step in range(ranks):
        place = (data - 1 - step) % ranks

        def piece(bit):
            own = lax.dynamic_slice(
                whole, (section, head ^ bit, place, 0, 0), (1, 1, 1, rows, columns)
            )[0, 0, 0]
            other = lax.dynamic_slice(
                whole, (1 - section, head ^ bit, place, 0, 0), (1, 1, 1, rows, columns)
            )[0, 0, 0]
            return add(own, flip(other, "section", 1)).astype(LOW)

        across = piece(3)
        upper = flip(across[:half], "tensor", 1)
        lower = flip(across[half:], "tensor", 2)
        near = piece(1)
        far = piece(2)
        far = jnp.concatenate([add(far[:half], upper).astype(LOW), far[half:]])
        near = jnp.concatenate([near[:half], add(near[half:], lower).astype(LOW)])
        total = add(piece(0), flip(near, "tensor", 1), flip(far, "tensor", 2))
        if arriving is not None:
            total = total + arriving.astype(WIDE)
        if step < ranks - 1:
            arriving = ring(total.astype(LOW), "fsdp")
    if spread:
        total = lax.psum_scatter(total.astype(LOW), "fsdp", scatter_dimension=0, tiled=True)
    return total.astype(WIDE)


def norm_rows(value_rows, gain_value):
    return (
        value_rows
        * lax.rsqrt(jnp.mean(value_rows * value_rows, axis=-1, keepdims=True) + EPSILON)
        * gain_value
    )


def norm_back(value_rows, gain_value, cotangent):
    scale = lax.rsqrt(jnp.mean(value_rows * value_rows, axis=-1, keepdims=True) + EPSILON)
    unit = value_rows * scale
    weighted = cotangent * gain_value
    rows_grad = scale * (weighted - unit * jnp.mean(weighted * unit, axis=-1, keepdims=True))
    gain_grad = jnp.sum(cotangent * unit, axis=0)
    return rows_grad, gain_grad


def turns(token_positions, head_width):
    half_depth = head_width // 2
    frequency = 10000.0 ** (-(jnp.arange(half_depth, dtype=WIDE) * 2.0) / head_width)
    turn = token_positions.astype(WIDE)[:, None] * frequency
    return jnp.cos(turn), jnp.sin(turn)


def rotate(value_rows, cosine, sine):
    half_depth = value_rows.shape[-1] // 2
    first = value_rows[..., :half_depth]
    second = value_rows[..., half_depth:]
    return jnp.concatenate(
        [first * cosine - second * sine, second * cosine + first * sine], axis=-1
    )


def gelu_parts(gate):
    root = (2.0 / jnp.pi) ** 0.5
    tanh = jnp.tanh(root * (gate + 0.044715 * gate * gate * gate))
    value = 0.5 * gate * (1.0 + tanh)
    slope = 0.5 * (1.0 + tanh) + 0.5 * gate * (1.0 - tanh * tanh) * root * (
        1.0 + 3.0 * 0.044715 * gate * gate
    )
    return value, slope


def keys_of(normed, layer, cosine, sine):
    key_raw = dot(normed, layer["key"])
    key_rows = rotate(norm_rows(key_raw, layer["key_gain"]), cosine, sine).astype(LOW)
    value_rows = dot(normed, layer["value"]).astype(LOW)
    return key_raw, key_rows, value_rows


def layer_forward(x, earlier, layer, allowed, window_turns):
    rows = x.shape[0]
    head_width = layer["key"].shape[1]
    heads = len(layer["query"])
    scale = head_width ** (-0.5)
    window_cos, window_sin = window_turns
    cosine, sine = window_cos[-rows:], window_sin[-rows:]
    normed = norm_rows(x, layer["before_gain"]).astype(LOW)
    if earlier is not None:
        everyone = jnp.concatenate(
            [norm_rows(earlier.astype(WIDE), layer["before_gain"]).astype(LOW), normed]
        )
        key_raw, key_rows, value_rows = keys_of(everyone, layer, window_cos, window_sin)
        key_raw = key_raw[-rows:]
    else:
        key_raw, own_keys, own_values = keys_of(normed, layer, cosine, sine)
        pair = jnp.concatenate([own_keys, own_values], axis=1)
        back = window_cos.shape[0] // rows - 1
        pair = jnp.concatenate([shifted(pair, "tensor", by) for by in range(back, 0, -1)] + [pair])
        key_rows, value_rows = pair[:, :head_width], pair[:, head_width:]
    query_raw, queries, chances, attended = [], [], [], []
    attention_sum = 0.0
    for head in range(heads):
        raw = dot(normed, layer["query"][head])
        query = rotate(norm_rows(raw, layer["query_gain"]), cosine, sine).astype(LOW)
        scores = jnp.where(allowed, dot_nt(query, key_rows) * scale, -1e30)
        exponent = jnp.exp(scores - jnp.max(scores, axis=-1, keepdims=True))
        chance = exponent / jnp.sum(exponent, axis=-1, keepdims=True)
        mixed = dot(chance.astype(LOW), value_rows).astype(LOW)
        attention_sum = attention_sum + dot_nt(mixed, layer["output"][head])
        query_raw.append(raw)
        queries.append(query)
        chances.append(chance)
        attended.append(mixed)
    hidden = x + norm_rows(attention_sum, layer["after_gain"])
    feed_in = norm_rows(hidden, layer["feed_gain"]).astype(LOW)
    gates, ups, products = [], [], []
    branch = 0.0
    for part in range(len(layer["gate"])):
        gate = dot(feed_in, layer["gate"][part])
        up = dot(feed_in, layer["up"][part])
        product = (gelu_parts(gate)[0] * up).astype(LOW)
        branch = branch + dot_nt(product, layer["down"][part])
        gates.append(gate)
        ups.append(up)
        products.append(product)
    result = hidden + norm_rows(branch, layer["final_gain"])
    kept = (
        x, normed, key_raw, key_rows, value_rows, query_raw, queries, chances, attended,
        attention_sum, hidden, feed_in, gates, ups, products, branch,
    )
    return result, kept


def layer_backward(dy, kept, layer, window_turns):
    (
        x, normed, key_raw, key_rows, value_rows, query_raw, queries, chances, attended,
        attention_sum, hidden, feed_in, gates, ups, products, branch,
    ) = kept
    rows = x.shape[0]
    head_width = layer["key"].shape[1]
    heads = len(layer["query"])
    scale = head_width ** (-0.5)
    window_cos, window_sin = window_turns
    cosine, sine = window_cos[-rows:], window_sin[-rows:]
    back = window_cos.shape[0] // rows - 1
    grads = {}
    d_branch, grads["final_gain"] = norm_back(branch, layer["final_gain"], dy)
    d_branch = d_branch.astype(LOW)
    d_feed = 0.0
    grads["gate"], grads["up"], grads["down"] = [], [], []
    for part in range(len(gates)):
        d_product = dot(d_branch, layer["down"][part])
        value, slope = gelu_parts(gates[part])
        d_gate = (d_product * ups[part] * slope).astype(LOW)
        d_up = (d_product * value).astype(LOW)
        d_feed = d_feed + dot_nt(d_gate, layer["gate"][part]) + dot_nt(d_up, layer["up"][part])
        grads["down"].append(dot_tn(d_branch, products[part]).astype(LOW))
        grads["gate"].append(dot_tn(feed_in, d_gate).astype(LOW))
        grads["up"].append(dot_tn(feed_in, d_up).astype(LOW))
    part_hidden, grads["feed_gain"] = norm_back(hidden, layer["feed_gain"], d_feed)
    d_hidden = dy + part_hidden
    d_sum, grads["after_gain"] = norm_back(attention_sum, layer["after_gain"], d_hidden)
    d_sum = d_sum.astype(LOW)
    d_keys, d_values = 0.0, 0.0
    d_normed = 0.0
    query_gain = 0.0
    grads["query"], grads["output"] = [], []
    for head in range(heads):
        d_mixed = dot(d_sum, layer["output"][head]).astype(LOW)
        grads["output"].append(dot_tn(d_sum, attended[head]).astype(LOW))
        chance = chances[head]
        d_chance = dot_nt(d_mixed, value_rows)
        weighted = jnp.sum(chance * d_chance, axis=-1, keepdims=True)
        d_scores = (chance * (d_chance - weighted)).astype(LOW)
        d_values = d_values + dot_tn(chance.astype(LOW), d_mixed)
        d_keys = d_keys + dot_tn(d_scores, queries[head]) * scale
        d_query = rotate(dot(d_scores, key_rows) * scale, cosine, -sine)
        d_raw, gain_part = norm_back(query_raw[head], layer["query_gain"], d_query)
        d_raw = d_raw.astype(LOW)
        query_gain = query_gain + gain_part
        grads["query"].append(dot_tn(normed, d_raw).astype(LOW))
        d_normed = d_normed + dot_nt(d_raw, layer["query"][head])
    grads["query_gain"] = query_gain
    pair = jnp.concatenate([d_keys, d_values], axis=1)
    own = pair[-rows:]
    for by in range(1, back + 1):
        first = (back - by) * rows
        own = own + shifted(pair[first : first + rows].astype(LOW), "tensor", -by).astype(WIDE)
    d_keys, d_values = own[:, :head_width], own[:, head_width:].astype(LOW)
    d_keys, grads["key_gain"] = norm_back(
        key_raw, layer["key_gain"], rotate(d_keys, cosine, -sine)
    )
    d_keys = d_keys.astype(LOW)
    grads["key"] = dot_tn(normed, d_keys).astype(LOW)
    grads["value"] = dot_tn(normed, d_values).astype(LOW)
    d_normed = d_normed + dot_nt(d_keys, layer["key"]) + dot_nt(d_values, layer["value"])
    part_inputs, grads["before_gain"] = norm_back(x, layer["before_gain"], d_normed)
    return d_hidden + part_inputs, grads


GAINS = ("before_gain", "query_gain", "key_gain", "after_gain", "feed_gain", "final_gain")


def body(
    inputs,
    out_grad,
    segment_ids,
    positions,
    before_gain,
    query_matrix,
    key_matrix,
    value_matrix,
    query_gain,
    key_gain,
    output_matrix,
    after_gain,
    feed_gain,
    gate_matrix,
    up_matrix,
    down_matrix,
    final_gain,
):
    section = lax.axis_index("section")
    data = lax.axis_index("fsdp")
    head = lax.axis_index("tensor")
    ranks = lax.axis_size("fsdp")
    heads = lax.axis_size("tensor")
    rows, width = inputs.shape[1:]
    head_width = key_matrix.shape[2]
    depth = gate_matrix.shape[1]
    piece_width = head_width // heads
    hidden_width = gate_matrix.shape[2]
    back = min(-(-(WINDOW - 1) // rows), heads - 1)

    own_key = lax.dynamic_slice_in_dim(key_matrix[0], head * piece_width, piece_width, 1)
    own_value = lax.dynamic_slice_in_dim(value_matrix[0], head * piece_width, piece_width, 1)
    slab = jnp.concatenate(
        [
            query_matrix[0],
            gate_matrix[0],
            up_matrix[0],
            down_matrix[0].T,
            output_matrix[0].T,
            own_key,
            own_value,
        ],
        axis=1,
    )
    widths = (
        head_width, hidden_width, hidden_width, hidden_width, head_width, piece_width, piece_width,
    )
    starts = [0]
    for step in widths:
        starts.append(starts[-1] + step)

    gain_list = (before_gain, query_gain, key_gain, after_gain, feed_gain, final_gain)
    gain_flat = jnp.concatenate([gain[0] for gain in gain_list])
    gain_all = lax.all_gather(gain_flat, ("section", "fsdp"), axis=0, tiled=False)
    gain_all = gain_all.reshape(2, ranks, -1).astype(WIDE)

    first_input = lax.dynamic_index_in_dim(inputs, section, 0, keepdims=False)
    last_cot = lax.dynamic_index_in_dim(out_grad, section, 0, keepdims=False)
    segments = lax.dynamic_index_in_dim(segment_ids, section, 0, keepdims=False)
    token_positions = lax.dynamic_index_in_dim(positions, section, 0, keepdims=False)
    earlier = jnp.concatenate([shifted(first_input, "tensor", by) for by in range(back, 0, -1)])
    padded_segments = jnp.concatenate([jnp.full((back * rows,), -1, jnp.int32), segments])
    padded_positions = jnp.concatenate([jnp.zeros((back * rows,), jnp.int32), token_positions])
    key_segments = lax.dynamic_slice_in_dim(padded_segments, head * rows, (back + 1) * rows)
    key_positions = lax.dynamic_slice_in_dim(padded_positions, head * rows, (back + 1) * rows)
    gap = key_positions[-rows:, None] - key_positions[None, :]
    allowed = (
        (key_segments[-rows:, None] == key_segments[None, :]) & (gap >= 0) & (gap < WINDOW)
    )
    window_turns = turns(key_positions, head_width)

    whole = gather_slabs(slab)
    layers = []
    for index in range(2):
        parts = [whole[index, t].reshape(ranks * depth, slab.shape[1]) for t in range(heads)]
        cut = [[part[:, a:b] for a, b in zip(starts[:-1], starts[1:])] for part in parts]
        layer = {
            "query": [c[0] for c in cut],
            "gate": [c[1] for c in cut],
            "up": [c[2] for c in cut],
            "down": [c[3] for c in cut],
            "output": [c[4] for c in cut],
            "key": jnp.concatenate([c[5] for c in cut], axis=1),
            "value": jnp.concatenate([c[6] for c in cut], axis=1),
        }
        first = 0
        for name, gain in zip(GAINS, gain_list):
            size = gain.shape[1]
            layer[name] = gain_all[index, :, first : first + size].reshape(-1)
            first += size
        layers.append(layer)

    out_first, kept_first = layer_forward(
        first_input.astype(WIDE), earlier, layers[0], allowed, window_turns
    )
    out_first = out_first.astype(LOW)
    out_second, kept_second = layer_forward(
        out_first.astype(WIDE), None, layers[1], allowed, window_turns
    )
    out_second = out_second.astype(LOW)
    grad_second, grads_second = layer_backward(
        last_cot.astype(WIDE), kept_second, layers[1], window_turns
    )
    grad_first, grads_first = layer_backward(
        grad_second.astype(LOW).astype(WIDE), kept_first, layers[0], window_turns
    )

    def settle(first, second):
        own = jnp.where(section == 0, first, second)
        sent = jnp.where(section == 0, second, first)
        other = flip(sent, "section", 1)
        return jnp.where(
            section == 0, jnp.stack([own, other]), jnp.stack([other, own])
        )[None]

    layer_out = settle(out_first, out_second)
    input_grad = settle(grad_first, grad_second)

    both = []
    gain_sums = []
    for grads in (grads_first, grads_second):
        per_head = []
        for t in range(heads):
            columns = slice(t * piece_width, (t + 1) * piece_width)
            per_head.append(
                jnp.concatenate(
                    [
                        grads["query"][t],
                        grads["gate"][t],
                        grads["up"][t],
                        grads["down"][t],
                        grads["output"][t],
                        grads["key"][:, columns],
                        grads["value"][:, columns],
                    ],
                    axis=1,
                ).reshape(ranks, depth, -1)
            )
        both.append(jnp.stack(per_head))
        gain_sums.append(
            jnp.concatenate([grads[name].reshape(ranks, -1) for name in GAINS], axis=1)
        )
    gain_sum = lax.psum(jnp.stack(gain_sums), ("section", "fsdp", "tensor"))
    gain_own = lax.dynamic_slice(gain_sum, (section, data, 0), (1, 1, gain_sum.shape[2]))[0]
    gain_grads = {}
    first = 0
    for name, gain in zip(GAINS, gain_list):
        size = gain.shape[1]
        gain_grads[name] = gain_own[:, first : first + size]
        first += size

    own = scatter_slabs(jnp.stack(both))
    cut = [own[:, a:b] for a, b in zip(starts[:-1], starts[1:])]
    pair = jnp.concatenate(cut[5:], axis=1).astype(LOW)
    shared = jnp.zeros((heads,) + pair.shape, LOW)
    for bit in range(heads):
        piece = pair if bit == 0 else flip(pair, "tensor", bit)
        shared = lax.dynamic_update_slice(shared, piece[None], (head ^ bit, 0, 0))
    shared = shared.astype(WIDE)
    key_grad = jnp.concatenate([shared[t, :, :piece_width] for t in range(heads)], axis=1)
    value_grad = jnp.concatenate([shared[t, :, piece_width:] for t in range(heads)], axis=1)
    return (
        layer_out,
        input_grad,
        gain_grads["before_gain"],
        cut[0][None],
        key_grad[None],
        value_grad[None],
        gain_grads["query_gain"],
        gain_grads["key_gain"],
        cut[4].T[None],
        gain_grads["after_gain"],
        gain_grads["feed_gain"],
        cut[1][None],
        cut[2][None],
        cut[3].T[None],
        gain_grads["final_gain"],
    )


def solution(mesh):
    in_specs = (
        P(None, ("fsdp", "tensor"), None),
        P(None, ("fsdp", "tensor"), None),
        P(None, "fsdp"),
        P(None, "fsdp"),
        P("section", "fsdp"),
        P("section", "fsdp", "tensor"),
        P("section", "fsdp", None),
        P("section", "fsdp", None),
        P("section", "fsdp"),
        P("section", "fsdp"),
        P("section", "tensor", "fsdp"),
        P("section", "fsdp"),
        P("section", "fsdp"),
        P("section", "fsdp", "tensor"),
        P("section", "fsdp", "tensor"),
        P("section", "tensor", "fsdp"),
        P("section", "fsdp"),
    )
    out_specs = (
        P("section", None, ("fsdp", "tensor"), None),
        P("section", None, ("fsdp", "tensor"), None),
        P("section", "fsdp"),
        P("section", "fsdp", "tensor"),
        P("section", "fsdp", None),
        P("section", "fsdp", None),
        P("section", "fsdp"),
        P("section", "fsdp"),
        P("section", "tensor", "fsdp"),
        P("section", "fsdp"),
        P("section", "fsdp"),
        P("section", "fsdp", "tensor"),
        P("section", "fsdp", "tensor"),
        P("section", "tensor", "fsdp"),
        P("section", "fsdp"),
    )
    return jax.shard_map(body, mesh=mesh, in_specs=in_specs, out_specs=out_specs, check_vma=False)
```

```python
import jax
import jax.numpy as jnp
from jax import lax
from jax.experimental import pallas as pl
from jax.experimental.pallas import tpu as pltpu
from jax.sharding import PartitionSpec as P

WINDOW = 512
EPSILON = 1e-06
LOW = jnp.bfloat16
WIDE = jnp.float32
SECTION = "section"
DATA = "fsdp"
HEAD = "tensor"
CORES = 2
HEADS = 4
VMEM_BYTES = 56 * 1024 * 1024


def flip(value, axis, bit):
    count = lax.axis_size(axis)
    return lax.ppermute(value, axis, [(i, i ^ bit) for i in range(count)])


def ring(value):
    count = lax.axis_size(DATA)
    return lax.ppermute(value, DATA, [(i, (i + 1) % count) for i in range(count)])


def shifted(value, axis, by):
    count = lax.axis_size(axis)
    pairs = [(i, i + by) for i in range(count) if 0 <= i + by < count]
    return lax.ppermute(value, axis, pairs)


def add(*parts):
    total = parts[0].astype(WIDE)
    for part in parts[1:]:
        total = total + part.astype(WIDE)
    return total


def dot(left, right):
    return jnp.dot(left, right, preferred_element_type=WIDE)


def dot_nt(left, right):
    return lax.dot_general(left, right, (((1,), (1,)), ((), ())), preferred_element_type=WIDE)


def dot_tn(left, right):
    return lax.dot_general(left, right, (((0,), (0,)), ((), ())), preferred_element_type=WIDE)


def gather_slab(slab):
    ranks = lax.axis_size(DATA)
    section = lax.axis_index(SECTION)
    data = lax.axis_index(DATA)
    head = lax.axis_index(HEAD)
    rows, columns = slab.shape
    cut = (columns // 256 + 1) * 128
    current = slab[None]
    if ranks > 4:
        current = lax.all_gather(slab, DATA, axis=0, tiled=False)
        steps, data = 1, 0
    else:
        steps = ranks
    whole = jnp.zeros((HEADS, ranks, CORES, rows, columns), slab.dtype)
    for step in range(steps):
        chunk = current
        place = (data - step) % steps
        if step < steps - 1:
            current = ring(current)
        near = flip(chunk, HEAD, 1)
        far = flip(chunk, HEAD, 2)
        across = jnp.concatenate(
            [flip(far[..., :cut], HEAD, 1), flip(near[..., cut:], HEAD, 2)], axis=-1
        )
        for piece, bit in ((chunk, 0), (near, 1), (far, 2), (across, 3)):
            other = flip(piece, SECTION, 1)
            for part, core in ((piece, section), (other, 1 - section)):
                whole = lax.dynamic_update_slice(
                    whole, part[None, :, None], (head ^ bit, place, core, 0, 0)
                )
    return whole.reshape(HEADS, ranks * CORES * rows, columns)


def scatter_slab(whole, ranks):
    section = lax.axis_index(SECTION)
    data = lax.axis_index(DATA)
    head = lax.axis_index(HEAD)
    columns = whole.shape[-1]
    rows = whole.shape[1] // (CORES * ranks)
    whole = whole.reshape(HEADS, ranks, CORES, rows, columns)
    cut = (columns // 256 + 1) * 128
    spread = ranks > 4
    steps = 1 if spread else ranks
    data = 0 if spread else data
    depth = ranks if spread else 1
    arriving = None
    total = None
    for step in range(steps):
        place = (data - 1 - step) % steps

        def piece(bit):
            own, other = (
                lax.dynamic_slice(
                    whole, (head ^ bit, place, core, 0, 0), (1, depth, 1, rows, columns)
                )[0, :, 0]
                for core in (section, 1 - section)
            )
            return add(own, flip(other, SECTION, 1)).astype(LOW)

        across = piece(3)
        left = flip(across[..., :cut], HEAD, 1)
        right = flip(across[..., cut:], HEAD, 2)
        near = piece(1)
        far = piece(2)
        far = jnp.concatenate([add(far[..., :cut], left).astype(LOW), far[..., cut:]], axis=-1)
        near = jnp.concatenate([near[..., :cut], add(near[..., cut:], right).astype(LOW)], axis=-1)
        total = add(piece(0), flip(near, HEAD, 1), flip(far, HEAD, 2))
        if arriving is not None:
            total = total + arriving.astype(WIDE)
        if step < steps - 1:
            arriving = ring(total.astype(LOW))
    if spread:
        return lax.psum_scatter(
            total.astype(LOW), DATA, scatter_dimension=0, tiled=False
        ).astype(WIDE)
    return total[0]


def by_section(own, other):
    section = lax.axis_index(SECTION)
    return jnp.where(section == 0, own, other), jnp.where(section == 0, other, own)


def gather_gains(gains):
    ranks = lax.axis_size(DATA)
    data = lax.axis_index(DATA)
    if ranks > 4:
        full = lax.all_gather(gains, DATA, axis=0, tiled=False)
    else:
        full = jnp.zeros((ranks,) + gains.shape, gains.dtype)
        for step in range(ranks):
            full = lax.dynamic_update_slice(full, gains[None], ((data - step) % ranks, 0))
            if step < ranks - 1:
                gains = ring(gains)
    return by_section(full, flip(full, SECTION, 1))


def scatter_gains(first, second):
    ranks = lax.axis_size(DATA)
    data = lax.axis_index(DATA)
    own, sent = by_section(first, second)
    total = own + flip(sent, SECTION, 1)
    total = total + flip(total, HEAD, 1)
    total = total + flip(total, HEAD, 2)
    if ranks > 4:
        return lax.psum_scatter(total, DATA, scatter_dimension=0, tiled=False)
    arriving = None
    for step in range(ranks):
        kept = lax.dynamic_index_in_dim(total, (data - 1 - step) % ranks, 0, keepdims=False)
        if arriving is not None:
            kept = kept + arriving
        if step < ranks - 1:
            arriving = ring(kept)
    return kept


def norm_parts(value_rows):
    scale = lax.rsqrt(jnp.mean(value_rows * value_rows, axis=-1, keepdims=True) + EPSILON)
    return value_rows * scale, scale


def norm_rows(value_rows, gain_value):
    return norm_parts(value_rows)[0] * gain_value


def norm_back(value_rows, gain_value, cotangent):
    unit, scale = norm_parts(value_rows)
    weighted = cotangent * gain_value
    rows_grad = scale * (weighted - unit * jnp.mean(weighted * unit, axis=-1, keepdims=True))
    return rows_grad, jnp.sum(cotangent * unit, axis=0, keepdims=True)


def rotate(value_rows, cosine, sine):
    half_depth = value_rows.shape[-1] // 2
    first = value_rows[:, :half_depth]
    second = value_rows[:, half_depth:]
    return jnp.concatenate(
        [first * cosine - second * sine, second * cosine + first * sine], axis=-1
    )


def gelu_parts(gate):
    root = 0.7978845608028654
    tanh = jnp.tanh(root * (gate + 0.044715 * gate * gate * gate))
    value = 0.5 * gate * (1.0 + tanh)
    slope = 0.5 * (1.0 + tanh) + 0.5 * gate * (1.0 - tanh * tanh) * root * (
        1.0 + 3.0 * 0.044715 * gate * gate
    )
    return value, slope


def softmax(scores):
    exponent = jnp.exp(scores - jnp.max(scores, axis=-1, keepdims=True))
    return exponent / jnp.sum(exponent, axis=-1, keepdims=True)


def shapes(slab_columns, width_pair):
    head_width = width_pair // 2
    hidden = (slab_columns - width_pair - width_pair // HEADS) // 3
    return head_width, hidden


def keys_kernel(x_ref, gain_ref, key_gain_ref, cos_ref, sin_ref, slab_ref, pair_ref, weights, sem):
    width_pair = pair_ref.shape[1]
    quarter = width_pair // HEADS
    copies = []
    for t in range(HEADS):
        copies.append(
            pltpu.make_async_copy(
                slab_ref.at[t, :, pl.ds(width_pair, quarter)],
                weights.at[:, pl.ds(t * quarter, quarter)],
                sem.at[t],
            )
        )
        copies[-1].start()
    normed = norm_rows(x_ref[...].astype(WIDE), gain_ref[...]).astype(LOW)
    for copy in copies:
        copy.wait()
    pair = dot(normed, weights[...])
    half = width_pair // 2
    key = rotate(norm_rows(pair[:, :half], key_gain_ref[...]), cos_ref[...], sin_ref[...])
    pair_ref[:, :half] = key.astype(LOW)
    pair_ref[:, half:] = pair[:, half:].astype(LOW)


def fetch_layer(slab_ref, attn, feed, sems):
    own = attn.shape[2]
    rest = feed.shape[2]
    first, second = [], []
    for t in range(HEADS):
        first.append(
            pltpu.make_async_copy(slab_ref.at[t, :, pl.ds(0, own)], attn.at[t], sems.at[t])
        )
        second.append(
            pltpu.make_async_copy(
                slab_ref.at[t, :, pl.ds(slab_ref.shape[2] - rest, rest)],
                feed.at[t],
                sems.at[HEADS + t],
            )
        )
    return first, second


def forward_kernel(
    x_ref, pair_ref, bias_ref, cos_ref, sin_ref, before_ref, query_gain_ref, after_ref,
    feed_gain_ref, final_ref, slab_ref,
    result_ref, attended_ref, sum_ref, hidden_ref, branch_ref,
    attn, feed, sems,
):
    width = pair_ref.shape[1] // 2
    hidden_width = feed.shape[2] // 3
    scale = width ** (-0.5)
    first, second = fetch_layer(slab_ref, attn, feed, sems)
    for copy in first + second:
        copy.start()
    x = x_ref[...].astype(WIDE)
    cosine, sine, bias = cos_ref[...], sin_ref[...], bias_ref[...]
    normed = norm_rows(x, before_ref[...]).astype(LOW)
    for t in range(HEADS):
        first[t].wait()
        raw = dot(normed, attn[t, :, :width])
        query = rotate(norm_rows(raw, query_gain_ref[...]), cosine, sine).astype(LOW)
        chance = softmax(dot_nt(query, pair_ref[:, :width]) * scale + bias).astype(LOW)
        mixed = dot(chance, pair_ref[:, width:]).astype(LOW)
        attended_ref[:, t * width : (t + 1) * width] = mixed
        part = dot_nt(mixed, attn[t, :, width:])
        sum_ref[...] = part if t == 0 else sum_ref[...] + part
    hidden = x + norm_rows(sum_ref[...], after_ref[...])
    hidden_ref[...] = hidden
    feed_in = norm_rows(hidden, feed_gain_ref[...]).astype(LOW)
    for t in range(HEADS):
        second[t].wait()
        gate = dot(feed_in, feed[t, :, :hidden_width])
        up = dot(feed_in, feed[t, :, hidden_width : 2 * hidden_width])
        product = (gelu_parts(gate)[0] * up).astype(LOW)
        part = dot_nt(product, feed[t, :, 2 * hidden_width :])
        branch_ref[...] = part if t == 0 else branch_ref[...] + part
    result = hidden_ref[...] + norm_rows(branch_ref[...], final_ref[...])
    result_ref[...] = result.astype(LOW)


def backward_kernel(
    dy_ref, x_ref, pair_ref, bias_ref, cos_ref, sin_ref, before_ref, query_gain_ref, after_ref,
    feed_gain_ref, final_ref, attended_ref, sum_ref, hidden_ref, branch_ref, slab_ref,
    grad_ref, own_ref, sent_ref, normed_ref, d_hidden_ref, gains_ref,
    attn, feed, grad_attn, grad_feed, d_pair, sems,
):
    width = pair_ref.shape[1] // 2
    hidden_width = feed.shape[2] // 3
    rows = x_ref.shape[0]
    scale = width ** (-0.5)
    first, second = fetch_layer(slab_ref, attn, feed, sems)
    out_first, out_second = [], []
    for t in range(HEADS):
        out_first.append(
            pltpu.make_async_copy(
                grad_attn.at[t], grad_ref.at[t, :, pl.ds(0, 2 * width)], sems.at[2 * HEADS + t]
            )
        )
        out_second.append(
            pltpu.make_async_copy(
                grad_feed.at[t],
                grad_ref.at[t, :, pl.ds(slab_ref.shape[2] - feed.shape[2], feed.shape[2])],
                sems.at[3 * HEADS + t],
            )
        )
    for copy in second + first:
        copy.start()
    dy = dy_ref[...].astype(WIDE)
    d_branch, final_grad = norm_back(branch_ref[...], final_ref[...], dy)
    d_branch = d_branch.astype(LOW)
    hidden = hidden_ref[...]
    feed_in = norm_rows(hidden, feed_gain_ref[...]).astype(LOW)
    for t in range(HEADS):
        second[t].wait()
        gate = dot(feed_in, feed[t, :, :hidden_width])
        up = dot(feed_in, feed[t, :, hidden_width : 2 * hidden_width])
        value, slope = gelu_parts(gate)
        product = (value * up).astype(LOW)
        d_product = dot(d_branch, feed[t, :, 2 * hidden_width :])
        d_gate = (d_product * up * slope).astype(LOW)
        d_up = (d_product * value).astype(LOW)
        part = dot_nt(d_gate, feed[t, :, :hidden_width]) + dot_nt(
            d_up, feed[t, :, hidden_width : 2 * hidden_width]
        )
        normed_ref[...] = part if t == 0 else normed_ref[...] + part
        grad_feed[t, :, :hidden_width] = dot_tn(feed_in, d_gate).astype(LOW)
        grad_feed[t, :, hidden_width : 2 * hidden_width] = dot_tn(feed_in, d_up).astype(LOW)
        grad_feed[t, :, 2 * hidden_width :] = dot_tn(d_branch, product).astype(LOW)
        out_second[t].start()
    part_hidden, feed_grad = norm_back(hidden, feed_gain_ref[...], normed_ref[...])
    d_hidden = dy + part_hidden
    d_hidden_ref[...] = d_hidden
    d_sum, after_grad = norm_back(sum_ref[...], after_ref[...], d_hidden)
    d_sum = d_sum.astype(LOW)
    cosine, sine, bias = cos_ref[...], sin_ref[...], bias_ref[...]
    normed = norm_rows(x_ref[...].astype(WIDE), before_ref[...]).astype(LOW)
    query_grad = jnp.zeros((1, width), WIDE)
    for t in range(HEADS):
        first[t].wait()
        key = pair_ref[:, :width]
        raw = dot(normed, attn[t, :, :width])
        query = rotate(norm_rows(raw, query_gain_ref[...]), cosine, sine).astype(LOW)
        chance = softmax(dot_nt(query, key) * scale + bias)
        d_mixed = dot(d_sum, attn[t, :, width:]).astype(LOW)
        grad_attn[t, :, width:] = dot_tn(
            d_sum, attended_ref[:, t * width : (t + 1) * width]
        ).astype(LOW)
        d_chance = dot_nt(d_mixed, pair_ref[:, width:])
        weighted = jnp.sum(chance * d_chance, axis=-1, keepdims=True)
        d_scores = (chance * (d_chance - weighted)).astype(LOW)
        d_key = dot_tn(d_scores, query) * scale
        d_value = dot_tn(chance.astype(LOW), d_mixed)
        d_pair[:, :width] = d_key if t == 0 else d_pair[:, :width] + d_key
        d_pair[:, width:] = d_value if t == 0 else d_pair[:, width:] + d_value
        d_query = rotate(dot(d_scores, key) * scale, cosine, -sine)
        d_raw, gain_part = norm_back(raw, query_gain_ref[...], d_query)
        query_grad = query_grad + gain_part
        d_raw = d_raw.astype(LOW)
        grad_attn[t, :, :width] = dot_tn(normed, d_raw).astype(LOW)
        out_first[t].start()
        part = dot_nt(d_raw, attn[t, :, :width])
        normed_ref[...] = part if t == 0 else normed_ref[...] + part
    earlier = d_pair.shape[0] - rows
    own_ref[...] = d_pair[earlier:, :]
    sent_ref[...] = d_pair[:earlier, :].astype(LOW)
    gains_ref[...] = jnp.zeros(gains_ref.shape, WIDE)
    gains_ref[0:1, :] = after_grad
    gains_ref[1:2, :] = feed_grad
    gains_ref[2:3, :] = final_grad
    gains_ref[3:4, :width] = query_grad
    for copy in out_first + out_second:
        copy.wait()


def closing_kernel(
    own_ref, arrived_ref, x_ref, before_ref, key_gain_ref, cos_ref, sin_ref, d_normed_ref,
    d_hidden_ref, slab_ref, grad_in_ref,
    input_ref, gains_ref, grad_ref,
    weights, grad_pair, sems,
):
    width_pair = own_ref.shape[1]
    quarter = width_pair // HEADS
    half = width_pair // 2
    copies, outs = [], []
    for t in range(HEADS):
        columns = pl.ds(t * quarter, quarter)
        copies.append(
            pltpu.make_async_copy(
                slab_ref.at[t, :, pl.ds(width_pair, quarter)], weights.at[:, columns], sems.at[t]
            )
        )
        outs.append(
            pltpu.make_async_copy(
                grad_pair.at[:, columns],
                grad_ref.at[t, :, pl.ds(width_pair, quarter)],
                sems.at[HEADS + t],
            )
        )
        copies[-1].start()
    x = x_ref[...].astype(WIDE)
    normed = norm_rows(x, before_ref[...]).astype(LOW)
    d_pair = own_ref[...]
    for back in range(arrived_ref.shape[0]):
        d_pair = d_pair + arrived_ref[back].astype(WIDE)
    for copy in copies:
        copy.wait()
    raw = dot(normed, weights[:, :half])
    d_key, key_grad = norm_back(
        raw, key_gain_ref[...], rotate(d_pair[:, :half], cos_ref[...], -sin_ref[...])
    )
    low_pair = jnp.concatenate([d_key.astype(LOW), d_pair[:, half:].astype(LOW)], axis=1)
    grad_pair[...] = dot_tn(normed, low_pair).astype(LOW)
    for copy in outs:
        copy.start()
    d_normed = d_normed_ref[...] + dot_nt(low_pair, weights[...])
    part_inputs, before_grad = norm_back(x, before_ref[...], d_normed)
    input_ref[...] = d_hidden_ref[...] + part_inputs
    gains_ref[...] = jnp.zeros(gains_ref.shape, WIDE)
    gains_ref[0:1, :] = before_grad
    gains_ref[1:2, :half] = key_grad
    for copy in outs:
        copy.wait()


def call(kernel, name, args, whole_at, outs, out_whole, scratch, sems, aliases=None):
    anywhere = pl.BlockSpec(memory_space=pl.ANY)
    near = pl.BlockSpec(memory_space=pltpu.VMEM)
    return pl.pallas_call(
        kernel,
        name=name,
        out_shape=[jax.ShapeDtypeStruct(shape, dtype) for shape, dtype in outs],
        in_specs=[anywhere if i in whole_at else near for i in range(len(args))],
        out_specs=[anywhere if i in out_whole else near for i in range(len(outs))],
        scratch_shapes=[pltpu.VMEM(shape, dtype) for shape, dtype in scratch]
        + [pltpu.SemaphoreType.DMA((sems,))],
        input_output_aliases=aliases or {},
        compiler_params=pltpu.CompilerParams(vmem_limit_bytes=VMEM_BYTES),
    )(*args)


def layer_keys(x, layer, turns):
    slab, before, query_gain, key_gain, after, feed_gain, final = layer
    pair = 2 * key_gain.shape[1]
    cosine, sine = turns
    args = (x, before, key_gain, cosine, sine, slab)
    outs = [((x.shape[0], pair), LOW)]
    scratch = [((x.shape[1], pair), LOW)]
    return call(keys_kernel, "keys", args, (5,), outs, (), scratch, HEADS)[0]


def layer_forward(x, pair, layer, bias, turns):
    slab, before, query_gain, key_gain, after, feed_gain, final = layer
    rows, width = x.shape
    own = pair.shape[1]
    rest = slab.shape[2] - own - own // HEADS
    args = (x, pair, bias) + turns + (before, query_gain, after, feed_gain, final, slab)
    token = ((rows, width), WIDE)
    outs = [((rows, width), LOW), ((rows, own // 2 * HEADS), LOW), token, token, token]
    scratch = [((HEADS, width, own), LOW), ((HEADS, width, rest), LOW)]
    return call(
        forward_kernel, "forward", args, (len(args) - 1,), outs, (), scratch, 2 * HEADS
    )


def layer_backward(dy, x, pair, kept, layer, bias, turns):
    slab, before, query_gain, key_gain, after, feed_gain, final = layer
    rows, width = x.shape
    own = pair.shape[1]
    rest = slab.shape[2] - own - own // HEADS
    earlier = pair.shape[0] - rows
    args = (
        (dy, x, pair, bias) + turns + (before, query_gain, after, feed_gain, final)
        + tuple(kept) + (slab,)
    )
    token = ((rows, width), WIDE)
    outs = [
        (slab.shape, LOW), ((rows, own), WIDE), ((earlier, own), LOW), token, token,
        ((8, width), WIDE),
    ]
    scratch = [
        ((HEADS, width, own), LOW), ((HEADS, width, rest), LOW),
        ((HEADS, width, own), LOW), ((HEADS, width, rest), LOW), (pair.shape, WIDE),
    ]
    grads, d_own, sent, d_normed, d_hidden, gains = call(
        backward_kernel, "backward", args, (len(args) - 1,), outs, (0,), scratch, 4 * HEADS
    )
    back = earlier // rows
    arrived = jnp.stack(
        [
            shifted(sent[(back - by) * rows : (back - by + 1) * rows], HEAD, -by)
            for by in range(1, back + 1)
        ]
    )
    args = (d_own, arrived, x, before, key_gain) + turns + (d_normed, d_hidden, slab, grads)
    outs = [token, ((8, width), WIDE), (slab.shape, LOW)]
    scratch = [((width, own), LOW), ((width, own), LOW)]
    input_grad, more, grads = call(
        closing_kernel, "closing", args, (9, 10), outs, (2,), scratch, 2 * HEADS, {10: 2}
    )
    gain_grads = (
        more[0], gains[3, : own // 2], more[1, : own // 2], gains[0], gains[1], gains[2],
    )
    return input_grad, grads, gain_grads


def body(
    inputs,
    out_grad,
    segment_ids,
    positions,
    before_gain,
    query_matrix,
    key_matrix,
    value_matrix,
    query_gain,
    key_gain,
    output_matrix,
    after_gain,
    feed_gain,
    gate_matrix,
    up_matrix,
    down_matrix,
    final_gain,
):
    section = lax.axis_index(SECTION)
    head = lax.axis_index(HEAD)
    ranks = lax.axis_size(DATA)
    rows, width = inputs.shape[1:]
    head_width = key_matrix.shape[2]
    depth = gate_matrix.shape[1]
    hidden_width = gate_matrix.shape[2]
    back = min(-(-(WINDOW - 1) // rows), HEADS - 1)
    quarter = 2 * head_width // HEADS

    shared = jnp.concatenate([key_matrix[0], value_matrix[0]], axis=1)
    slab = jnp.concatenate(
        [
            query_matrix[0],
            output_matrix[0].T,
            lax.dynamic_slice_in_dim(shared, head * quarter, quarter, 1),
            gate_matrix[0],
            up_matrix[0],
            down_matrix[0].T,
        ],
        axis=1,
    )
    half = depth // CORES
    upper, lower = slab[:half], slab[half:]
    traded = flip(jnp.where(section == 0, lower, upper), SECTION, 1)
    halves = jnp.where(section == 0, upper, traded), jnp.where(section == 0, traded, lower)

    gain_list = (before_gain, query_gain, key_gain, after_gain, feed_gain, final_gain)
    sizes = [gain.shape[1] for gain in gain_list]
    gain_both = gather_gains(jnp.concatenate([gain[0] for gain in gain_list]))

    first_input = lax.dynamic_index_in_dim(inputs, section, 0, keepdims=False)
    last_cot = lax.dynamic_index_in_dim(out_grad, section, 0, keepdims=False)
    segments = lax.dynamic_index_in_dim(segment_ids, section, 0, keepdims=False)
    token_positions = lax.dynamic_index_in_dim(positions, section, 0, keepdims=False)
    everyone = jnp.concatenate(
        [shifted(first_input, HEAD, by) for by in range(back, 0, -1)] + [first_input]
    )
    padded_segments = jnp.concatenate([jnp.full((back * rows,), -1, jnp.int32), segments])
    padded_positions = jnp.concatenate([jnp.zeros((back * rows,), jnp.int32), token_positions])
    key_segments = lax.dynamic_slice_in_dim(padded_segments, head * rows, (back + 1) * rows)
    key_positions = lax.dynamic_slice_in_dim(padded_positions, head * rows, (back + 1) * rows)
    gap = key_positions[-rows:, None] - key_positions[None, :]
    allowed = (
        (key_segments[-rows:, None] == key_segments[None, :]) & (gap >= 0) & (gap < WINDOW)
    )
    bias = jnp.where(allowed, 0.0, -1e30).astype(WIDE)
    half_depth = head_width // 2
    frequency = 10000.0 ** (-(jnp.arange(half_depth, dtype=WIDE) * 2.0) / head_width)
    turn = key_positions.astype(WIDE)[:, None] * frequency
    turns_all = jnp.cos(turn), jnp.sin(turn)
    turns = turns_all[0][-rows:], turns_all[1][-rows:]

    layers = []
    for index in range(2):
        gains, first = [], 0
        for size in sizes:
            gains.append(gain_both[index][:, first : first + size].reshape(1, -1).astype(WIDE))
            first += size
        layers.append((gather_slab(halves[index]),) + tuple(gains))

    pair_first = layer_keys(everyone, layers[0], turns_all)
    out_first, *kept_first = layer_forward(first_input, pair_first, layers[0], bias, turns)
    own_pair = layer_keys(out_first, layers[1], turns)
    pair_second = jnp.concatenate(
        [shifted(own_pair, HEAD, by) for by in range(back, 0, -1)] + [own_pair]
    )
    out_second, *kept_second = layer_forward(out_first, pair_second, layers[1], bias, turns)
    grad_second, slab_second, gains_second = layer_backward(
        last_cot, out_first, pair_second, kept_second, layers[1], bias, turns
    )
    total_second = scatter_slab(slab_second, ranks)
    grad_first, slab_first, gains_first = layer_backward(
        grad_second.astype(LOW), first_input, pair_first, kept_first, layers[0], bias, turns
    )
    total_first = scatter_slab(slab_first, ranks)

    def settle(first, second):
        own, sent = by_section(first, second)
        return jnp.stack(by_section(own, flip(sent, SECTION, 1)))[None]

    gain_own = scatter_gains(
        *(
            jnp.concatenate([gain.reshape(ranks, -1) for gain in gains], axis=1)
            for gains in (gains_first, gains_second)
        )
    )
    gain_grads, first = [], 0
    for size in sizes:
        gain_grads.append(gain_own[None, first : first + size])
        first += size

    own, sent = by_section(total_first, total_second)
    own = jnp.concatenate(by_section(own, flip(sent, SECTION, 1)))
    starts = [0]
    for step in (head_width, head_width, quarter, hidden_width, hidden_width, hidden_width):
        starts.append(starts[-1] + step)
    cut = [own[:, a:b] for a, b in zip(starts[:-1], starts[1:])]
    pair = cut[2].astype(LOW)
    shared = jnp.zeros((depth, 2 * head_width), LOW)
    for bit in range(HEADS):
        piece = pair if bit == 0 else flip(pair, HEAD, bit)
        shared = lax.dynamic_update_slice(shared, piece, (0, (head ^ bit) * quarter))
    shared = shared.astype(WIDE)
    return (
        settle(out_first, out_second),
        settle(grad_first, grad_second),
        gain_grads[0],
        cut[0][None],
        shared[None, :, :head_width],
        shared[None, :, head_width:],
        gain_grads[1],
        gain_grads[2],
        cut[1].T[None],
        gain_grads[3],
        gain_grads[4],
        cut[3][None],
        cut[4][None],
        cut[5].T[None],
        gain_grads[5],
    )


def solution(mesh):
    tokens = P(None, (DATA, HEAD), None)
    pack = P(None, DATA)
    gain = P(SECTION, DATA)
    split = P(SECTION, DATA, HEAD)
    plain = P(SECTION, DATA, None)
    turned = P(SECTION, HEAD, DATA)
    outs = P(SECTION, None, (DATA, HEAD), None)
    weights = (
        gain, split, plain, plain, gain, gain, turned, gain, gain, split, split, turned, gain,
    )
    return jax.shard_map(
        body,
        mesh=mesh,
        in_specs=(tokens, tokens, pack, pack) + weights,
        out_specs=(outs, outs) + weights,
        check_vma=False,
    )
```

```python
import functools

import jax
import jax.numpy as jnp
from jax import lax
from jax.experimental import pallas as pl
from jax.experimental.pallas import tpu as pltpu
from jax.sharding import PartitionSpec as P

WINDOW = 512
EPSILON = 1e-06
LOW = jnp.bfloat16
WIDE = jnp.float32
SECTION = "section"
DATA = "fsdp"
HEAD = "tensor"
CORES = 2
HEADS = 4
VMEM_BYTES = 56 * 1024 * 1024


def flip(value, axis, bit):
    count = lax.axis_size(axis)
    return lax.ppermute(value, axis, [(i, i ^ bit) for i in range(count)])


def ring(value):
    count = lax.axis_size(DATA)
    return lax.ppermute(value, DATA, [(i, (i + 1) % count) for i in range(count)])


def shifted(value, axis, by):
    count = lax.axis_size(axis)
    pairs = [(i, i + by) for i in range(count) if 0 <= i + by < count]
    return lax.ppermute(value, axis, pairs)


def add(*parts):
    total = parts[0].astype(WIDE)
    for part in parts[1:]:
        total = total + part.astype(WIDE)
    return total


def dot(left, right):
    return jnp.dot(left, right, preferred_element_type=WIDE)


def dot_nt(left, right):
    return lax.dot_general(left, right, (((1,), (1,)), ((), ())), preferred_element_type=WIDE)


def dot_tn(left, right):
    return lax.dot_general(left, right, (((0,), (0,)), ((), ())), preferred_element_type=WIDE)


def after(value, *others):
    anywhere = pl.BlockSpec(memory_space=pl.ANY)
    return pl.pallas_call(
        lambda *refs: None,
        name="after",
        out_shape=jax.ShapeDtypeStruct(value.shape, value.dtype),
        in_specs=[anywhere] * (1 + len(others)),
        out_specs=anywhere,
        input_output_aliases={0: 0},
    )(value, *others)


def gather_slab(slab):
    ranks = lax.axis_size(DATA)
    if ranks > 4:
        rows, columns = slab.shape
        chunk = lax.all_gather(slab, DATA, axis=0, tiled=False)
        near = flip(chunk, HEAD, 1)
        far = flip(chunk, HEAD, 2)
        piece = jnp.stack([chunk, near, far, flip(near, HEAD, 2)])
        both = jnp.stack(by_section(piece, flip(piece, SECTION, 1)), axis=2)
        return (both.reshape(HEADS, ranks * CORES * rows, columns),), [chunk] * 4
    pieces = ()
    chunks = [slab]
    for step in range(ranks):
        chunk = chunks[-1]
        if step < ranks - 1:
            chunks.append(ring(chunk))
        near = flip(chunk, HEAD, 1)
        far = flip(chunk, HEAD, 2)
        across = flip(far, HEAD, 1) if 2 * step < ranks else flip(near, HEAD, 2)
        own = jnp.stack([chunk, near, far, across])
        pieces += (own, flip(own, SECTION, 1))
    return pieces, chunks


def groups_of(ranks):
    return ((2, 3), (1, 0)) if ranks == 4 else (tuple(range(ranks - 1, -1, -1)),)


def first_sums(grads, ranks):
    if ranks > 4:
        section = lax.axis_index(SECTION)
        whole = jnp.concatenate(grads, axis=-1)
        rows = whole.shape[2] // (CORES * ranks)
        whole = whole.reshape(HEADS, ranks, CORES, rows, whole.shape[3])
        own = lax.dynamic_index_in_dim(whole, section, 2, keepdims=False)
        other = lax.dynamic_index_in_dim(whole, 1 - section, 2, keepdims=False)
        return [add(own, flip(other, SECTION, 1)).astype(LOW)]
    sums = []
    count = len(groups_of(ranks))
    own_pair, other_pair = grads[2 * count :]
    other_pair = flip(other_pair, SECTION, 1)
    first = 0
    for index, group in enumerate(groups_of(ranks)):
        own, other = grads[2 * index], grads[2 * index + 1]
        span = slice(first, first + len(group))
        first += len(group)
        sums.append(
            jnp.concatenate(
                [
                    add(own, flip(other, SECTION, 1)).astype(LOW),
                    add(own_pair[:, span], other_pair[:, span]).astype(LOW),
                ],
                axis=-1,
            )
        )
    return sums


def scatter_sums(sums, ranks):
    if ranks > 4:
        part = sums[0]
        part = add(part[:2], flip(part[2:], HEAD, 2))
        total = add(part[0], flip(part[1].astype(LOW), HEAD, 1))
        total = lax.psum_scatter(total.astype(LOW), DATA, scatter_dimension=0, tiled=False)
        return total.astype(WIDE), total
    kept = None
    mark = None
    for part, group in zip(sums, groups_of(ranks)):
        middle = len(group) // 2
        upper = flip(part[3, :middle], HEAD, 1)
        lower = flip(part[3, middle:], HEAD, 2)
        far = jnp.concatenate([add(part[2, :middle], upper).astype(LOW), part[2, middle:]])
        near = jnp.concatenate([part[1, :middle], add(part[1, middle:], lower).astype(LOW)])
        mark = near if mark is None else mark
        total = add(part[0], flip(near, HEAD, 1), flip(far, HEAD, 2))
        for place, distance in enumerate(group):
            piece = total[place]
            if distance:
                pairs = [(i, (i + distance) % ranks) for i in range(ranks)]
                piece = lax.ppermute(piece.astype(LOW), DATA, pairs)
            kept = piece.astype(WIDE) if kept is None else add(kept, piece)
    return kept, mark


def by_section(own, other):
    section = lax.axis_index(SECTION)
    return jnp.where(section == 0, own, other), jnp.where(section == 0, other, own)


def gather_gains(gains):
    ranks = lax.axis_size(DATA)
    data = lax.axis_index(DATA)
    if ranks > 4:
        full = lax.all_gather(gains, DATA, axis=0, tiled=False)
    else:
        full = jnp.zeros((ranks,) + gains.shape, gains.dtype)
        for step in range(ranks):
            full = lax.dynamic_update_slice(full, gains[None], ((data - step) % ranks, 0))
            if step < ranks - 1:
                gains = ring(gains)
    return by_section(full, flip(full, SECTION, 1))


def scatter_gains(first, second):
    ranks = lax.axis_size(DATA)
    data = lax.axis_index(DATA)
    own, sent = by_section(first, second)
    total = own + flip(sent, SECTION, 1)
    total = total + flip(total, HEAD, 1)
    total = total + flip(total, HEAD, 2)
    if ranks > 4:
        return lax.psum_scatter(total, DATA, scatter_dimension=0, tiled=False)
    arriving = None
    for step in range(ranks):
        kept = lax.dynamic_index_in_dim(total, (data - 1 - step) % ranks, 0, keepdims=False)
        if arriving is not None:
            kept = kept + arriving
        if step < ranks - 1:
            arriving = ring(kept)
    return kept


def norm_parts(value_rows):
    scale = lax.rsqrt(jnp.mean(value_rows * value_rows, axis=-1, keepdims=True) + EPSILON)
    return value_rows * scale, scale


def norm_rows(value_rows, gain_value):
    return norm_parts(value_rows)[0] * gain_value


def norm_back(value_rows, gain_value, cotangent):
    unit, scale = norm_parts(value_rows)
    weighted = cotangent * gain_value
    rows_grad = scale * (weighted - unit * jnp.mean(weighted * unit, axis=-1, keepdims=True))
    return rows_grad, jnp.sum(cotangent * unit, axis=0, keepdims=True)


def rotate(value_rows, cosine, sine):
    half_depth = value_rows.shape[-1] // 2
    first = value_rows[:, :half_depth]
    second = value_rows[:, half_depth:]
    return jnp.concatenate(
        [first * cosine - second * sine, second * cosine + first * sine], axis=-1
    )


def gelu_parts(gate):
    root = 0.7978845608028654
    tanh = jnp.tanh(root * (gate + 0.044715 * gate * gate * gate))
    value = 0.5 * gate * (1.0 + tanh)
    slope = 0.5 * (1.0 + tanh) + 0.5 * gate * (1.0 - tanh * tanh) * root * (
        1.0 + 3.0 * 0.044715 * gate * gate
    )
    return value, slope


def softmax(scores):
    exponent = jnp.exp(scores - jnp.max(scores, axis=-1, keepdims=True))
    return exponent / jnp.sum(exponent, axis=-1, keepdims=True)


def row_table(ranks, depth):
    section = lax.axis_index(SECTION)
    data = lax.axis_index(DATA)
    head = lax.axis_index(HEAD)
    half = depth // CORES
    cores = (section, 1 - section)
    if ranks > 4:
        rows = [jnp.int32(0)] * 3
    else:
        rows = [(data - k) % ranks * depth + core * half for k in range(ranks) for core in cores]
        groups = groups_of(ranks)
        order = [(group, core) for group in groups for core in cores]
        order += [(sum(groups, ()), core) for core in cores]
        for group, core in order:
            rows += [(data + k) % ranks * depth + core * half for k in group]
    return jnp.stack([jnp.int32(row) for row in rows] + [head ^ bit for bit in range(HEADS)])


def fetches(table, pieces, bit, source, target, sems):
    copies = []
    for i, piece in enumerate(pieces):
        rows = piece.shape[1]
        first = pl.multiple_of(table[i], 16)
        copies.append(
            pltpu.make_async_copy(
                piece.at[bit, :, pl.ds(*source)],
                target(pl.ds(first, rows)),
                sems.at[bit * len(pieces) + i],
            )
        )
        copies[-1].start()
    return copies


def sendings(table, first_entry, grads, bit, source, columns, sems):
    copies = []
    for grad in grads:
        for place in range(grad.shape[1]):
            rows = grad.shape[2]
            first = pl.multiple_of(table[first_entry + len(copies)], 16)
            copies.append(
                pltpu.make_async_copy(
                    source(pl.ds(first, rows)),
                    grad.at[bit, place, :, pl.ds(*columns)],
                    sems.at[len(copies)],
                )
            )
            copies[-1].start()
    return copies


def quarter_columns(table, bit, quarter):
    last = table.shape[0] - HEADS + bit
    return pl.ds(pl.multiple_of(table[last] * quarter, quarter), quarter)


def keys_kernel(count, table, x_ref, gain_ref, key_gain_ref, cos_ref, sin_ref, *refs):
    pieces = refs[:count]
    pair_ref, weights, sems = refs[count:]
    width_pair = pair_ref.shape[1]
    quarter = width_pair // HEADS
    copies = []
    for t in range(HEADS):
        columns = quarter_columns(table, t, quarter)
        copies += fetches(
            table, pieces, t, (width_pair, quarter), lambda rows: weights.at[rows, columns], sems
        )
    normed = norm_rows(x_ref[...].astype(WIDE), gain_ref[...]).astype(LOW)
    for copy in copies:
        copy.wait()
    pair = dot(normed, weights[...])
    half = width_pair // 2
    key = rotate(norm_rows(pair[:, :half], key_gain_ref[...]), cos_ref[...], sin_ref[...])
    pair_ref[:, :half] = key.astype(LOW)
    pair_ref[:, half:] = pair[:, half:].astype(LOW)


def fetch_attn(table, pieces, attn, sems):
    return [
        fetches(table, pieces, t, (0, attn.shape[2]), lambda rows: attn.at[t, rows, :], sems)
        for t in range(HEADS)
    ]


def fetch_feed(table, pieces, feed, sems):
    first = pieces[0].shape[2] - feed.shape[2]
    return [
        fetches(table, pieces, t, (first, feed.shape[2]), lambda rows: feed.at[t, rows, :], sems)
        for t in range(HEADS)
    ]


def wait_all(copies):
    for copy in copies:
        copy.wait()


def forward_kernel(
    count, table,
    x_ref, pair_ref, bias_ref, cos_ref, sin_ref, before_ref, query_gain_ref, after_ref,
    feed_gain_ref, final_ref, *refs,
):
    pieces = refs[:count]
    result_ref, attended_ref, sum_ref, hidden_ref, branch_ref, attn, feed, first_sems, second_sems = (
        refs[count:]
    )
    width = pair_ref.shape[1] // 2
    hidden_width = feed.shape[2] // 3
    scale = width ** (-0.5)
    first = fetch_attn(table, pieces, attn, first_sems)
    second = fetch_feed(table, pieces, feed, second_sems)
    x = x_ref[...].astype(WIDE)
    cosine, sine, bias = cos_ref[...], sin_ref[...], bias_ref[...]
    normed = norm_rows(x, before_ref[...]).astype(LOW)
    for t in range(HEADS):
        wait_all(first[t])
        raw = dot(normed, attn[t, :, :width])
        query = rotate(norm_rows(raw, query_gain_ref[...]), cosine, sine).astype(LOW)
        chance = softmax(dot_nt(query, pair_ref[:, :width]) * scale + bias).astype(LOW)
        mixed = dot(chance, pair_ref[:, width:]).astype(LOW)
        attended_ref[:, t * width : (t + 1) * width] = mixed
        part = dot_nt(mixed, attn[t, :, width:])
        sum_ref[...] = part if t == 0 else sum_ref[...] + part
    hidden = x + norm_rows(sum_ref[...], after_ref[...])
    hidden_ref[...] = hidden
    feed_in = norm_rows(hidden, feed_gain_ref[...]).astype(LOW)
    for t in range(HEADS):
        wait_all(second[t])
        gate = dot(feed_in, feed[t, :, :hidden_width])
        up = dot(feed_in, feed[t, :, hidden_width : 2 * hidden_width])
        product = (gelu_parts(gate)[0] * up).astype(LOW)
        part = dot_nt(product, feed[t, :, 2 * hidden_width :])
        branch_ref[...] = part if t == 0 else branch_ref[...] + part
    result = hidden_ref[...] + norm_rows(branch_ref[...], final_ref[...])
    result_ref[...] = result.astype(LOW)


def backward_kernel(
    count, grad_count, table,
    dy_ref, x_ref, pair_ref, bias_ref, cos_ref, sin_ref, before_ref, query_gain_ref, after_ref,
    feed_gain_ref, final_ref, attended_ref, sum_ref, hidden_ref, branch_ref, *refs,
):
    pieces = refs[:count]
    grads = refs[count : count + grad_count]
    own_ref, sent_ref, normed_ref, d_hidden_ref, gains_ref = refs[
        count + grad_count : count + grad_count + 5
    ]
    attn, feed, grad_attn, grad_feed, d_pair, first_sems, second_sems, *out_sems = refs[
        count + grad_count + 5 :
    ]
    entry = len(pieces)
    width = pair_ref.shape[1] // 2
    hidden_width = feed.shape[2] // 3
    rows = x_ref.shape[0]
    scale = width ** (-0.5)
    second = fetch_feed(table, pieces, feed, second_sems)
    first = fetch_attn(table, pieces, attn, first_sems)
    sent = []
    dy = dy_ref[...].astype(WIDE)
    d_branch, final_grad = norm_back(branch_ref[...], final_ref[...], dy)
    d_branch = d_branch.astype(LOW)
    hidden = hidden_ref[...]
    feed_in = norm_rows(hidden, feed_gain_ref[...]).astype(LOW)
    for t in range(HEADS):
        wait_all(second[t])
        gate = dot(feed_in, feed[t, :, :hidden_width])
        up = dot(feed_in, feed[t, :, hidden_width : 2 * hidden_width])
        value, slope = gelu_parts(gate)
        product = (value * up).astype(LOW)
        d_product = dot(d_branch, feed[t, :, 2 * hidden_width :])
        d_gate = (d_product * up * slope).astype(LOW)
        d_up = (d_product * value).astype(LOW)
        part = dot_nt(d_gate, feed[t, :, :hidden_width]) + dot_nt(
            d_up, feed[t, :, hidden_width : 2 * hidden_width]
        )
        normed_ref[...] = part if t == 0 else normed_ref[...] + part
        grad_feed[t, :, :hidden_width] = dot_tn(feed_in, d_gate).astype(LOW)
        grad_feed[t, :, hidden_width : 2 * hidden_width] = dot_tn(feed_in, d_up).astype(LOW)
        grad_feed[t, :, 2 * hidden_width :] = dot_tn(d_branch, product).astype(LOW)
        sent += sendings(
            table, entry, grads, t, lambda at: grad_feed.at[t, at, :],
            (2 * width, feed.shape[2]), out_sems[t],
        )
    part_hidden, feed_grad = norm_back(hidden, feed_gain_ref[...], normed_ref[...])
    d_hidden = dy + part_hidden
    d_hidden_ref[...] = d_hidden
    d_sum, after_grad = norm_back(sum_ref[...], after_ref[...], d_hidden)
    d_sum = d_sum.astype(LOW)
    cosine, sine, bias = cos_ref[...], sin_ref[...], bias_ref[...]
    normed = norm_rows(x_ref[...].astype(WIDE), before_ref[...]).astype(LOW)
    query_grad = jnp.zeros((1, width), WIDE)
    for t in range(HEADS):
        wait_all(first[t])
        key = pair_ref[:, :width]
        raw = dot(normed, attn[t, :, :width])
        query = rotate(norm_rows(raw, query_gain_ref[...]), cosine, sine).astype(LOW)
        chance = softmax(dot_nt(query, key) * scale + bias)
        d_mixed = dot(d_sum, attn[t, :, width:]).astype(LOW)
        grad_attn[t, :, width:] = dot_tn(
            d_sum, attended_ref[:, t * width : (t + 1) * width]
        ).astype(LOW)
        d_chance = dot_nt(d_mixed, pair_ref[:, width:])
        weighted = jnp.sum(chance * d_chance, axis=-1, keepdims=True)
        d_scores = (chance * (d_chance - weighted)).astype(LOW)
        d_key = dot_tn(d_scores, query) * scale
        d_value = dot_tn(chance.astype(LOW), d_mixed)
        d_pair[:, :width] = d_key if t == 0 else d_pair[:, :width] + d_key
        d_pair[:, width:] = d_value if t == 0 else d_pair[:, width:] + d_value
        d_query = rotate(dot(d_scores, key) * scale, cosine, -sine)
        d_raw, gain_part = norm_back(raw, query_gain_ref[...], d_query)
        query_grad = query_grad + gain_part
        d_raw = d_raw.astype(LOW)
        grad_attn[t, :, :width] = dot_tn(normed, d_raw).astype(LOW)
        sent += sendings(
            table, entry, grads, t, lambda at: grad_attn.at[t, at, :], (0, 2 * width),
            out_sems[HEADS + t],
        )
        part = dot_nt(d_raw, attn[t, :, :width])
        normed_ref[...] = part if t == 0 else normed_ref[...] + part
    earlier = d_pair.shape[0] - rows
    own_ref[...] = d_pair[earlier:, :]
    sent_ref[...] = d_pair[:earlier, :].astype(LOW)
    gains_ref[...] = jnp.zeros(gains_ref.shape, WIDE)
    gains_ref[0:1, :] = after_grad
    gains_ref[1:2, :] = feed_grad
    gains_ref[2:3, :] = final_grad
    gains_ref[3:4, :width] = query_grad
    wait_all(sent)


def closing_kernel(
    count, grad_count, table,
    own_ref, arrived_ref, x_ref, before_ref, key_gain_ref, cos_ref, sin_ref, d_normed_ref,
    d_hidden_ref, *refs,
):
    pieces = refs[:count]
    refs = refs[count:]
    grads = refs[:grad_count]
    input_ref, gains_ref, weights, grad_pair, sems, *out_sems = refs[grad_count:]
    width_pair = own_ref.shape[1]
    main = grads[0].shape[1] * len(grads)
    quarter = width_pair // HEADS
    half = width_pair // 2
    copies, sent = [], []
    for t in range(HEADS):
        columns = quarter_columns(table, t, quarter)
        copies += fetches(
            table, pieces, t, (width_pair, quarter), lambda rows: weights.at[rows, columns], sems
        )
    x = x_ref[...].astype(WIDE)
    normed = norm_rows(x, before_ref[...]).astype(LOW)
    d_pair = own_ref[...]
    for back in range(arrived_ref.shape[0]):
        d_pair = d_pair + arrived_ref[back].astype(WIDE)
    wait_all(copies)
    raw = dot(normed, weights[:, :half])
    d_key, key_grad = norm_back(
        raw, key_gain_ref[...], rotate(d_pair[:, :half], cos_ref[...], -sin_ref[...])
    )
    low_pair = jnp.concatenate([d_key.astype(LOW), d_pair[:, half:].astype(LOW)], axis=1)
    grad_pair[...] = dot_tn(normed, low_pair).astype(LOW)
    for t in range(HEADS):
        columns = quarter_columns(table, t, quarter)
        sent += sendings(
            table, len(pieces) + main, grads, t, lambda at: grad_pair.at[at, columns],
            (0, quarter), out_sems[t],
        )
    d_normed = d_normed_ref[...] + dot_nt(low_pair, weights[...])
    part_inputs, before_grad = norm_back(x, before_ref[...], d_normed)
    input_ref[...] = d_hidden_ref[...] + part_inputs
    gains_ref[...] = jnp.zeros(gains_ref.shape, WIDE)
    gains_ref[0:1, :] = before_grad
    gains_ref[1:2, :half] = key_grad
    wait_all(sent)


def call(kernel, name, args, far_args, outs, far_outs, scratch, sems, cost, aliases=None):
    anywhere = pl.BlockSpec(memory_space=pl.ANY)
    near = pl.BlockSpec(memory_space=pltpu.VMEM)
    flops, moved = cost
    return pl.pallas_call(
        kernel,
        name=name,
        out_shape=[jax.ShapeDtypeStruct(shape, dtype) for shape, dtype in far_outs + outs],
        in_specs=[pl.BlockSpec(memory_space=pltpu.SMEM)]
        + [near] * (len(args) - 1)
        + [anywhere] * len(far_args),
        out_specs=[anywhere] * len(far_outs) + [near] * len(outs),
        scratch_shapes=[pltpu.VMEM(shape, dtype) for shape, dtype in scratch]
        + [pltpu.SemaphoreType.DMA((count,)) for count in sems],
        input_output_aliases=aliases or {},
        cost_estimate=pl.CostEstimate(flops=flops, transcendentals=0, bytes_accessed=moved),
        compiler_params=pltpu.CompilerParams(vmem_limit_bytes=VMEM_BYTES),
    )(*args, *far_args)


def layer_keys(x, layer, turns, table):
    pieces, before, query_gain, key_gain, after_gain, feed_gain, final = layer
    far = tuple(pieces)
    pair = 2 * key_gain.shape[1]
    rows, width = x.shape
    args = (table, x, before, key_gain) + turns
    kernel = functools.partial(keys_kernel, len(far))
    cost = (2 * rows * width * pair, 2 * width * pair)
    outs = [((rows, pair), LOW)]
    return call(kernel, "keys", args, far, outs, [], [((width, pair), LOW)], [HEADS * len(far)], cost)[0]


def sizes_of(pieces, own):
    columns = pieces[0].shape[2]
    rest = columns - own - own // HEADS
    return columns, rest


def layer_forward(x, pair, layer, bias, turns, table):
    pieces, before, query_gain, key_gain, after_gain, feed_gain, final = layer
    far = tuple(pieces)
    rows, width = x.shape
    own = pair.shape[1]
    columns, rest = sizes_of(pieces, own)
    args = (table, x, pair, bias) + turns + (before, query_gain, after_gain, feed_gain, final)
    token = ((rows, width), WIDE)
    outs = [((rows, width), LOW), ((rows, own // 2 * HEADS), LOW), token, token, token]
    scratch = [((HEADS, width, own), LOW), ((HEADS, width, rest), LOW)]
    kernel = functools.partial(forward_kernel, len(far))
    cost = (4 * rows * width * columns * HEADS, 2 * width * columns * HEADS)
    return call(kernel, "forward", args, far, outs, [], scratch, [HEADS * len(far)] * 2, cost)


def layer_backward(dy, x, pair, kept, layer, bias, turns, table, ranks):
    pieces, before, query_gain, key_gain, after_gain, feed_gain, final = layer
    far = tuple(pieces)
    rows, width = x.shape
    own = pair.shape[1]
    columns, rest = sizes_of(pieces, own)
    earlier = pair.shape[0] - rows
    args = (
        (table, dy, x, pair, bias) + turns + (before, query_gain, after_gain, feed_gain, final)
        + tuple(kept)
    )
    token = ((rows, width), WIDE)
    if ranks > 4:
        grad_shapes = [((HEADS, 1, width, own + rest), LOW)]
        pair_shapes = [((HEADS, 1, width, own // HEADS), LOW)]
    else:
        half = width // (ranks * CORES)
        grad_shapes = [
            ((HEADS, len(group), half, own + rest), LOW)
            for group in groups_of(ranks)
            for core in range(CORES)
        ]
        pair_shapes = [((HEADS, ranks, half, own // HEADS), LOW)] * CORES
    count = sum(shape[1] for shape, dtype in grad_shapes)
    outs = [((rows, own), WIDE), ((earlier, own), LOW), token, token, ((8, width), WIDE)]
    scratch = [
        ((HEADS, width, own), LOW), ((HEADS, width, rest), LOW),
        ((HEADS, width, own), LOW), ((HEADS, width, rest), LOW), (pair.shape, WIDE),
    ]
    kernel = functools.partial(backward_kernel, len(far), len(grad_shapes))
    cost = (8 * rows * width * columns * HEADS, 4 * width * columns * HEADS)
    result = call(
        kernel, "backward", args, far, outs, grad_shapes, scratch,
        [HEADS * len(far)] * 2 + [count] * 2 * HEADS, cost,
    )
    grads = tuple(result[: len(grad_shapes)])
    d_own, sent, d_normed, d_hidden, gains = result[len(grad_shapes) :]
    back = earlier // rows
    arrived = jnp.stack(
        [
            shifted(sent[(back - by) * rows : (back - by + 1) * rows], HEAD, -by)
            for by in range(1, back + 1)
        ]
    )
    args = (table, d_own, arrived, x, before, key_gain) + turns + (d_normed, d_hidden)
    outs = [token, ((8, width), WIDE)]
    scratch = [((width, own), LOW), ((width, own), LOW)]
    kernel = functools.partial(closing_kernel, len(far), len(pair_shapes))
    cost = (6 * rows * width * own, 4 * width * own)
    result = call(
        kernel, "closing", args, far, outs, pair_shapes, scratch,
        [HEADS * len(far)] + [count] * HEADS, cost,
    )
    input_grad, more = result[len(pair_shapes) :]
    gain_grads = (
        more[0], gains[3, : own // 2], more[1, : own // 2], gains[0], gains[1], gains[2],
    )
    return input_grad, grads + tuple(result[: len(pair_shapes)]), gain_grads


def body(
    inputs,
    out_grad,
    segment_ids,
    positions,
    before_gain,
    query_matrix,
    key_matrix,
    value_matrix,
    query_gain,
    key_gain,
    output_matrix,
    after_gain,
    feed_gain,
    gate_matrix,
    up_matrix,
    down_matrix,
    final_gain,
):
    section = lax.axis_index(SECTION)
    head = lax.axis_index(HEAD)
    ranks = lax.axis_size(DATA)
    rows, width = inputs.shape[1:]
    head_width = key_matrix.shape[2]
    depth = gate_matrix.shape[1]
    hidden_width = gate_matrix.shape[2]
    back = min(-(-(WINDOW - 1) // rows), HEADS - 1)
    quarter = 2 * head_width // HEADS

    shared = jnp.concatenate([key_matrix[0], value_matrix[0]], axis=1)
    slab = jnp.concatenate(
        [
            query_matrix[0],
            output_matrix[0].T,
            lax.dynamic_slice_in_dim(shared, head * quarter, quarter, 1),
            gate_matrix[0],
            up_matrix[0],
            down_matrix[0].T,
        ],
        axis=1,
    )
    half = depth // CORES
    upper, lower = slab[:half], slab[half:]
    traded = flip(jnp.where(section == 0, lower, upper), SECTION, 1)
    halves = jnp.where(section == 0, upper, traded), jnp.where(section == 0, traded, lower)

    first_pieces, chunks = gather_slab(halves[0])
    second_pieces, unused = gather_slab(after(halves[1], chunks[3]))
    pieces = first_pieces, second_pieces

    gain_list = (before_gain, query_gain, key_gain, after_gain, feed_gain, final_gain)
    sizes = [gain.shape[1] for gain in gain_list]
    gain_both = gather_gains(
        after(jnp.concatenate([gain[0] for gain in gain_list]), chunks[2])
    )

    first_input = lax.dynamic_index_in_dim(inputs, section, 0, keepdims=False)
    last_cot = lax.dynamic_index_in_dim(out_grad, section, 0, keepdims=False)
    segments = lax.dynamic_index_in_dim(segment_ids, section, 0, keepdims=False)
    token_positions = lax.dynamic_index_in_dim(positions, section, 0, keepdims=False)
    everyone = jnp.concatenate(
        [shifted(after(first_input, chunks[1]), HEAD, by) for by in range(back, 0, -1)] + [first_input]
    )
    padded_segments = jnp.concatenate([jnp.full((back * rows,), -1, jnp.int32), segments])
    padded_positions = jnp.concatenate([jnp.zeros((back * rows,), jnp.int32), token_positions])
    key_segments = lax.dynamic_slice_in_dim(padded_segments, head * rows, (back + 1) * rows)
    key_positions = lax.dynamic_slice_in_dim(padded_positions, head * rows, (back + 1) * rows)
    gap = key_positions[-rows:, None] - key_positions[None, :]
    allowed = (
        (key_segments[-rows:, None] == key_segments[None, :]) & (gap >= 0) & (gap < WINDOW)
    )
    bias = jnp.where(allowed, 0.0, -1e30).astype(WIDE)
    half_depth = head_width // 2
    frequency = 10000.0 ** (-(jnp.arange(half_depth, dtype=WIDE) * 2.0) / head_width)
    turn = key_positions.astype(WIDE)[:, None] * frequency
    turns_all = jnp.cos(turn), jnp.sin(turn)
    turns = turns_all[0][-rows:], turns_all[1][-rows:]

    layers = []
    for index in range(2):
        gains, first = [], 0
        for size in sizes:
            gains.append(gain_both[index][:, first : first + size].reshape(1, -1).astype(WIDE))
            first += size
        layers.append((pieces[index],) + tuple(gains))

    table = row_table(ranks, depth)
    pair_first = layer_keys(everyone, layers[0], turns_all, table)
    out_first, *kept_first = layer_forward(first_input, pair_first, layers[0], bias, turns, table)
    own_pair = layer_keys(out_first, layers[1], turns, table)
    pair_second = jnp.concatenate(
        [shifted(own_pair, HEAD, by) for by in range(back, 0, -1)] + [own_pair]
    )
    out_second, *kept_second = layer_forward(
        out_first, pair_second, layers[1], bias, turns, table
    )
    grad_second, slab_second, gains_second = layer_backward(
        last_cot, out_first, pair_second, kept_second, layers[1], bias, turns, table, ranks
    )
    sums_second = first_sums(slab_second, ranks)
    grad_first, slab_first, gains_first = layer_backward(
        after(grad_second.astype(LOW), *sums_second), first_input, pair_first, kept_first, layers[0], bias, turns, table, ranks
    )
    total_second, unused = scatter_sums(sums_second, ranks)
    total_first, mark = scatter_sums(first_sums(slab_first, ranks), ranks)

    def settle(first, second):
        own, sent = by_section(first, second)
        return jnp.stack(by_section(own, flip(sent, SECTION, 1)))[None]

    gain_own = scatter_gains(
        *(
            after(jnp.concatenate([gain.reshape(ranks, -1) for gain in gains], axis=1), mark)
            for gains in (gains_first, gains_second)
        )
    )
    gain_grads, first = [], 0
    for size in sizes:
        gain_grads.append(gain_own[None, first : first + size])
        first += size

    own, sent = by_section(total_first, total_second)
    own = jnp.concatenate(by_section(own, flip(sent, SECTION, 1)))
    starts = [0]
    for step in (head_width, head_width, hidden_width, hidden_width, hidden_width, quarter):
        starts.append(starts[-1] + step)
    cut = [own[:, a:b] for a, b in zip(starts[:-1], starts[1:])]
    pair = cut[5].astype(LOW)
    shared = jnp.zeros((depth, 2 * head_width), LOW)
    for bit in range(HEADS):
        piece = pair if bit == 0 else flip(pair, HEAD, bit)
        shared = lax.dynamic_update_slice(shared, piece, (0, (head ^ bit) * quarter))
    shared = shared.astype(WIDE)
    return (
        settle(out_first, out_second),
        settle(grad_first, grad_second),
        gain_grads[0],
        cut[0][None],
        shared[None, :, :head_width],
        shared[None, :, head_width:],
        gain_grads[1],
        gain_grads[2],
        cut[1].T[None],
        gain_grads[3],
        gain_grads[4],
        cut[2][None],
        cut[3][None],
        cut[4].T[None],
        gain_grads[5],
    )


def solution(mesh):
    tokens = P(None, (DATA, HEAD), None)
    pack = P(None, DATA)
    gain = P(SECTION, DATA)
    split = P(SECTION, DATA, HEAD)
    plain = P(SECTION, DATA, None)
    turned = P(SECTION, HEAD, DATA)
    outs = P(SECTION, None, (DATA, HEAD), None)
    weights = (
        gain, split, plain, plain, gain, gain, turned, gain, gain, split, split, turned, gain,
    )
    return jax.shard_map(
        body,
        mesh=mesh,
        in_specs=(tokens, tokens, pack, pack) + weights,
        out_specs=(outs, outs) + weights,
        check_vma=False,
    )
```

```python
import functools

import jax
import jax.numpy as jnp
from jax import lax
from jax.experimental import pallas as pl
from jax.experimental.pallas import tpu as pltpu
from jax.sharding import PartitionSpec as P

WINDOW = 512
EPSILON = 1e-06
LOW = jnp.bfloat16
WIDE = jnp.float32
SECTION = "section"
DATA = "fsdp"
HEAD = "tensor"
CORES = 2
HEADS = 4
EXTRA = 128
VMEM_BYTES = 56 * 1024 * 1024


def flip(value, axis, bit):
    count = lax.axis_size(axis)
    return lax.ppermute(value, axis, [(i, i ^ bit) for i in range(count)])


def ring(value):
    count = lax.axis_size(DATA)
    return lax.ppermute(value, DATA, [(i, (i + 1) % count) for i in range(count)])


def shifted(value, axis, by):
    count = lax.axis_size(axis)
    pairs = [(i, i + by) for i in range(count) if 0 <= i + by < count]
    return lax.ppermute(value, axis, pairs)


def add(*parts):
    total = parts[0].astype(WIDE)
    for part in parts[1:]:
        total = total + part.astype(WIDE)
    return total


def dot(left, right):
    return jnp.dot(left, right, preferred_element_type=WIDE)


def dot_nt(left, right):
    return lax.dot_general(left, right, (((1,), (1,)), ((), ())), preferred_element_type=WIDE)


def dot_tn(left, right):
    return lax.dot_general(left, right, (((0,), (0,)), ((), ())), preferred_element_type=WIDE)


def after(value, *others):
    anywhere = pl.BlockSpec(memory_space=pl.ANY)
    return pl.pallas_call(
        lambda *refs: None,
        name="after",
        out_shape=jax.ShapeDtypeStruct(value.shape, value.dtype),
        in_specs=[anywhere] * (1 + len(others)),
        out_specs=anywhere,
        input_output_aliases={0: 0},
    )(value, *others)


def gather_slab(slab):
    ranks = lax.axis_size(DATA)
    if ranks > 4:
        rows, columns = slab.shape
        chunk = lax.all_gather(slab, DATA, axis=0, tiled=False)
        near = flip(chunk, HEAD, 1)
        far = flip(chunk, HEAD, 2)
        piece = jnp.stack([chunk, near, far, flip(near, HEAD, 2)])
        both = jnp.stack(by_section(piece, flip(piece, SECTION, 1)), axis=2)
        return (both.reshape(HEADS, ranks * CORES * rows, columns),), [chunk] * 4
    pieces = ()
    chunks = [slab]
    for step in range(ranks):
        chunk = chunks[-1]
        if step < ranks - 1:
            chunks.append(ring(chunk))
        near = flip(chunk, HEAD, 1)
        far = flip(chunk, HEAD, 2)
        across = flip(far, HEAD, 1) if 2 * step < ranks else flip(near, HEAD, 2)
        own = jnp.stack([chunk, near, far, across])
        pieces += (own, flip(own, SECTION, 1))
    return pieces, chunks


def groups_of(ranks):
    return ((2, 3), (1, 0)) if ranks == 4 else (tuple(range(ranks - 1, -1, -1)),)


def first_sums(grads, ranks):
    if ranks > 4:
        section = lax.axis_index(SECTION)
        whole = jnp.concatenate(grads, axis=-1)
        rows = whole.shape[2] // (CORES * ranks)
        whole = whole.reshape(HEADS, ranks, CORES, rows, whole.shape[3])
        own = lax.dynamic_index_in_dim(whole, section, 2, keepdims=False)
        other = lax.dynamic_index_in_dim(whole, 1 - section, 2, keepdims=False)
        return [add(own, flip(other, SECTION, 1)).astype(LOW)]
    sums = []
    count = len(groups_of(ranks))
    own_pair, other_pair = grads[2 * count :]
    other_pair = flip(other_pair, SECTION, 1)
    first = 0
    for index, group in enumerate(groups_of(ranks)):
        own, other = grads[2 * index], grads[2 * index + 1]
        span = slice(first, first + len(group))
        first += len(group)
        sums.append(
            jnp.concatenate(
                [
                    add(own, flip(other, SECTION, 1)).astype(LOW),
                    add(own_pair[:, span], other_pair[:, span]).astype(LOW),
                ],
                axis=-1,
            )
        )
    return sums


def scatter_sums(sums, ranks):
    if ranks > 4:
        part = sums[0]
        part = add(part[:2], flip(part[2:], HEAD, 2))
        total = add(part[0], flip(part[1].astype(LOW), HEAD, 1))
        total = lax.psum_scatter(total.astype(LOW), DATA, scatter_dimension=0, tiled=False)
        return total.astype(WIDE), total
    kept = None
    mark = None
    for part, group in zip(sums, groups_of(ranks)):
        middle = len(group) // 2
        upper = flip(part[3, :middle], HEAD, 1)
        lower = flip(part[3, middle:], HEAD, 2)
        far = jnp.concatenate([add(part[2, :middle], upper).astype(LOW), part[2, middle:]])
        near = jnp.concatenate([part[1, :middle], add(part[1, middle:], lower).astype(LOW)])
        mark = near if mark is None else mark
        total = add(part[0], flip(near, HEAD, 1), flip(far, HEAD, 2))
        for place, distance in enumerate(group):
            piece = total[place]
            if distance:
                pairs = [(i, (i + distance) % ranks) for i in range(ranks)]
                piece = lax.ppermute(piece.astype(LOW), DATA, pairs)
            kept = piece.astype(WIDE) if kept is None else add(kept, piece)
    return kept, mark


def by_section(own, other):
    section = lax.axis_index(SECTION)
    return jnp.where(section == 0, own, other), jnp.where(section == 0, other, own)


def gains_in(pieces, count, first):
    ranks = lax.axis_size(DATA)
    data = lax.axis_index(DATA)
    full = jnp.zeros((ranks, count), LOW)
    for step in range(ranks):
        lines = pieces[2 * step][0, : count // EXTRA, first : first + EXTRA]
        full = lax.dynamic_update_slice(full, lines.reshape(1, -1), ((data - step) % ranks, 0))
    return full


def gather_gains(gains):
    ranks = lax.axis_size(DATA)
    data = lax.axis_index(DATA)
    if ranks > 4:
        full = lax.all_gather(gains, DATA, axis=0, tiled=False)
    else:
        full = jnp.zeros((ranks,) + gains.shape, gains.dtype)
        for step in range(ranks):
            full = lax.dynamic_update_slice(full, gains[None], ((data - step) % ranks, 0))
            if step < ranks - 1:
                gains = ring(gains)
    return by_section(full, flip(full, SECTION, 1))


def gains_beside(pairs, gains, ranks):
    data = lax.axis_index(DATA)
    width = pairs[0].shape[-1]
    rows = pairs[0].shape[2]
    gains = gains.reshape(ranks, -1, 128).astype(LOW)
    gains = jnp.pad(gains, ((0, 0), (0, rows - gains.shape[1]), (0, 0)))
    order = sum(groups_of(ranks), ())
    block = jnp.stack(
        [lax.dynamic_index_in_dim(gains, (data + k) % ranks, 0, keepdims=False) for k in order]
    )
    block = jnp.broadcast_to(block, (HEADS,) + block.shape)
    return tuple(jnp.concatenate([pair, block], axis=-1) for pair in pairs)


def scatter_gains(first, second):
    ranks = lax.axis_size(DATA)
    data = lax.axis_index(DATA)
    own, sent = by_section(first, second)
    total = own + flip(sent, SECTION, 1)
    total = total + flip(total, HEAD, 1)
    total = total + flip(total, HEAD, 2)
    if ranks > 4:
        return lax.psum_scatter(total, DATA, scatter_dimension=0, tiled=False)
    arriving = None
    for step in range(ranks):
        kept = lax.dynamic_index_in_dim(total, (data - 1 - step) % ranks, 0, keepdims=False)
        if arriving is not None:
            kept = kept + arriving
        if step < ranks - 1:
            arriving = ring(kept)
    return kept


def norm_parts(value_rows):
    scale = lax.rsqrt(jnp.mean(value_rows * value_rows, axis=-1, keepdims=True) + EPSILON)
    return value_rows * scale, scale


def norm_rows(value_rows, gain_value):
    return norm_parts(value_rows)[0] * gain_value


def norm_back(value_rows, gain_value, cotangent):
    unit, scale = norm_parts(value_rows)
    weighted = cotangent * gain_value
    rows_grad = scale * (weighted - unit * jnp.mean(weighted * unit, axis=-1, keepdims=True))
    return rows_grad, jnp.sum(cotangent * unit, axis=0, keepdims=True)


def rotate(value_rows, cosine, sine):
    half_depth = value_rows.shape[-1] // 2
    first = value_rows[:, :half_depth]
    second = value_rows[:, half_depth:]
    return jnp.concatenate(
        [first * cosine - second * sine, second * cosine + first * sine], axis=-1
    )


def gelu_parts(gate):
    root = 0.7978845608028654
    tanh = jnp.tanh(root * (gate + 0.044715 * gate * gate * gate))
    value = 0.5 * gate * (1.0 + tanh)
    slope = 0.5 * (1.0 + tanh) + 0.5 * gate * (1.0 - tanh * tanh) * root * (
        1.0 + 3.0 * 0.044715 * gate * gate
    )
    return value, slope


def softmax(scores):
    exponent = jnp.exp(scores - jnp.max(scores, axis=-1, keepdims=True))
    return exponent / jnp.sum(exponent, axis=-1, keepdims=True)


def row_table(ranks, depth):
    section = lax.axis_index(SECTION)
    data = lax.axis_index(DATA)
    head = lax.axis_index(HEAD)
    half = depth // CORES
    cores = (section, 1 - section)
    if ranks > 4:
        rows = [jnp.int32(0)] * 3
    else:
        rows = [(data - k) % ranks * depth + core * half for k in range(ranks) for core in cores]
        groups = groups_of(ranks)
        order = [(group, core) for group in groups for core in cores]
        order += [(sum(groups, ()), core) for core in cores]
        for group, core in order:
            rows += [(data + k) % ranks * depth + core * half for k in group]
    return jnp.stack([jnp.int32(row) for row in rows] + [head ^ bit for bit in range(HEADS)])


def fetches(table, pieces, bit, source, target, sems):
    copies = []
    for i, piece in enumerate(pieces):
        rows = piece.shape[1]
        first = pl.multiple_of(table[i], 16)
        copies.append(
            pltpu.make_async_copy(
                piece.at[bit, :, pl.ds(*source)],
                target(pl.ds(first, rows)),
                sems.at[bit * len(pieces) + i],
            )
        )
        copies[-1].start()
    return copies


def sendings(table, first_entry, grads, bit, source, columns, sems):
    copies = []
    for grad in grads:
        for place in range(grad.shape[1]):
            rows = grad.shape[2]
            first = pl.multiple_of(table[first_entry + len(copies)], 16)
            copies.append(
                pltpu.make_async_copy(
                    source(pl.ds(first, rows)),
                    grad.at[bit, place, :, pl.ds(*columns)],
                    sems.at[len(copies)],
                )
            )
            copies[-1].start()
    return copies


def quarter_columns(table, bit, quarter):
    last = table.shape[0] - HEADS + bit
    return pl.ds(pl.multiple_of(table[last] * quarter, quarter), quarter)


def keys_kernel(count, table, x_ref, gain_ref, key_gain_ref, cos_ref, sin_ref, *refs):
    pieces = refs[:count]
    pair_ref, weights, sems = refs[count:]
    width_pair = pair_ref.shape[1]
    quarter = width_pair // HEADS
    copies = []
    for t in range(HEADS):
        columns = quarter_columns(table, t, quarter)
        copies += fetches(
            table, pieces, t, (width_pair, quarter), lambda rows: weights.at[rows, columns], sems
        )
    normed = norm_rows(x_ref[...].astype(WIDE), gain_ref[...]).astype(LOW)
    for copy in copies:
        copy.wait()
    pair = dot(normed, weights[...])
    half = width_pair // 2
    key = rotate(norm_rows(pair[:, :half], key_gain_ref[...]), cos_ref[...], sin_ref[...])
    pair_ref[:, :half] = key.astype(LOW)
    pair_ref[:, half:] = pair[:, half:].astype(LOW)


def fetch_attn(table, pieces, attn, sems):
    return [
        fetches(table, pieces, t, (0, attn.shape[2]), lambda rows: attn.at[t, rows, :], sems)
        for t in range(HEADS)
    ]


def fetch_feed(table, pieces, feed, sems):
    first = pieces[0].shape[2] - feed.shape[2]
    return [
        fetches(table, pieces, t, (first, feed.shape[2]), lambda rows: feed.at[t, rows, :], sems)
        for t in range(HEADS)
    ]


def wait_all(copies):
    for copy in copies:
        copy.wait()


def forward_kernel(
    count, table,
    x_ref, pair_ref, bias_ref, cos_ref, sin_ref, before_ref, query_gain_ref, after_ref,
    feed_gain_ref, final_ref, *refs,
):
    pieces = refs[:count]
    result_ref, attended_ref, sum_ref, hidden_ref, branch_ref, attn, feed, first_sems, second_sems = (
        refs[count:]
    )
    width = pair_ref.shape[1] // 2
    hidden_width = feed.shape[2] // 3
    scale = width ** (-0.5)
    first = fetch_attn(table, pieces, attn, first_sems)
    second = fetch_feed(table, pieces, feed, second_sems)
    x = x_ref[...].astype(WIDE)
    cosine, sine, bias = cos_ref[...], sin_ref[...], bias_ref[...]
    normed = norm_rows(x, before_ref[...]).astype(LOW)
    for t in range(HEADS):
        wait_all(first[t])
        raw = dot(normed, attn[t, :, :width])
        query = rotate(norm_rows(raw, query_gain_ref[...]), cosine, sine).astype(LOW)
        chance = softmax(dot_nt(query, pair_ref[:, :width]) * scale + bias).astype(LOW)
        mixed = dot(chance, pair_ref[:, width:]).astype(LOW)
        attended_ref[:, t * width : (t + 1) * width] = mixed
        part = dot_nt(mixed, attn[t, :, width:])
        sum_ref[...] = part if t == 0 else sum_ref[...] + part
    hidden = x + norm_rows(sum_ref[...], after_ref[...])
    hidden_ref[...] = hidden
    feed_in = norm_rows(hidden, feed_gain_ref[...]).astype(LOW)
    for t in range(HEADS):
        wait_all(second[t])
        gate = dot(feed_in, feed[t, :, :hidden_width])
        up = dot(feed_in, feed[t, :, hidden_width : 2 * hidden_width])
        product = (gelu_parts(gate)[0] * up).astype(LOW)
        part = dot_nt(product, feed[t, :, 2 * hidden_width :])
        branch_ref[...] = part if t == 0 else branch_ref[...] + part
    result = hidden_ref[...] + norm_rows(branch_ref[...], final_ref[...])
    result_ref[...] = result.astype(LOW)


def backward_kernel(
    count, grad_count, table,
    dy_ref, x_ref, pair_ref, bias_ref, cos_ref, sin_ref, before_ref, query_gain_ref, after_ref,
    feed_gain_ref, final_ref, attended_ref, sum_ref, hidden_ref, branch_ref, *refs,
):
    pieces = refs[:count]
    grads = refs[count : count + grad_count]
    own_ref, sent_ref, normed_ref, d_hidden_ref, gains_ref = refs[
        count + grad_count : count + grad_count + 5
    ]
    attn, feed, grad_attn, grad_feed, d_pair, first_sems, second_sems, *out_sems = refs[
        count + grad_count + 5 :
    ]
    entry = len(pieces)
    width = pair_ref.shape[1] // 2
    hidden_width = feed.shape[2] // 3
    rows = x_ref.shape[0]
    scale = width ** (-0.5)
    second = fetch_feed(table, pieces, feed, second_sems)
    first = fetch_attn(table, pieces, attn, first_sems)
    sent = []
    dy = dy_ref[...].astype(WIDE)
    d_branch, final_grad = norm_back(branch_ref[...], final_ref[...], dy)
    d_branch = d_branch.astype(LOW)
    hidden = hidden_ref[...]
    feed_in = norm_rows(hidden, feed_gain_ref[...]).astype(LOW)
    for t in range(HEADS):
        wait_all(second[t])
        gate = dot(feed_in, feed[t, :, :hidden_width])
        up = dot(feed_in, feed[t, :, hidden_width : 2 * hidden_width])
        value, slope = gelu_parts(gate)
        product = (value * up).astype(LOW)
        d_product = dot(d_branch, feed[t, :, 2 * hidden_width :])
        d_gate = (d_product * up * slope).astype(LOW)
        d_up = (d_product * value).astype(LOW)
        part = dot_nt(d_gate, feed[t, :, :hidden_width]) + dot_nt(
            d_up, feed[t, :, hidden_width : 2 * hidden_width]
        )
        normed_ref[...] = part if t == 0 else normed_ref[...] + part
        grad_feed[t, :, :hidden_width] = dot_tn(feed_in, d_gate).astype(LOW)
        grad_feed[t, :, hidden_width : 2 * hidden_width] = dot_tn(feed_in, d_up).astype(LOW)
        grad_feed[t, :, 2 * hidden_width :] = dot_tn(d_branch, product).astype(LOW)
        sent += sendings(
            table, entry, grads, t, lambda at: grad_feed.at[t, at, :],
            (2 * width, feed.shape[2]), out_sems[t],
        )
    part_hidden, feed_grad = norm_back(hidden, feed_gain_ref[...], normed_ref[...])
    d_hidden = dy + part_hidden
    d_hidden_ref[...] = d_hidden
    d_sum, after_grad = norm_back(sum_ref[...], after_ref[...], d_hidden)
    d_sum = d_sum.astype(LOW)
    cosine, sine, bias = cos_ref[...], sin_ref[...], bias_ref[...]
    normed = norm_rows(x_ref[...].astype(WIDE), before_ref[...]).astype(LOW)
    query_grad = jnp.zeros((1, width), WIDE)
    for t in range(HEADS):
        wait_all(first[t])
        key = pair_ref[:, :width]
        raw = dot(normed, attn[t, :, :width])
        query = rotate(norm_rows(raw, query_gain_ref[...]), cosine, sine).astype(LOW)
        chance = softmax(dot_nt(query, key) * scale + bias)
        d_mixed = dot(d_sum, attn[t, :, width:]).astype(LOW)
        grad_attn[t, :, width:] = dot_tn(
            d_sum, attended_ref[:, t * width : (t + 1) * width]
        ).astype(LOW)
        d_chance = dot_nt(d_mixed, pair_ref[:, width:])
        weighted = jnp.sum(chance * d_chance, axis=-1, keepdims=True)
        d_scores = (chance * (d_chance - weighted)).astype(LOW)
        d_key = dot_tn(d_scores, query) * scale
        d_value = dot_tn(chance.astype(LOW), d_mixed)
        d_pair[:, :width] = d_key if t == 0 else d_pair[:, :width] + d_key
        d_pair[:, width:] = d_value if t == 0 else d_pair[:, width:] + d_value
        d_query = rotate(dot(d_scores, key) * scale, cosine, -sine)
        d_raw, gain_part = norm_back(raw, query_gain_ref[...], d_query)
        query_grad = query_grad + gain_part
        d_raw = d_raw.astype(LOW)
        grad_attn[t, :, :width] = dot_tn(normed, d_raw).astype(LOW)
        sent += sendings(
            table, entry, grads, t, lambda at: grad_attn.at[t, at, :], (0, 2 * width),
            out_sems[HEADS + t],
        )
        part = dot_nt(d_raw, attn[t, :, :width])
        normed_ref[...] = part if t == 0 else normed_ref[...] + part
    earlier = d_pair.shape[0] - rows
    own_ref[...] = d_pair[earlier:, :]
    sent_ref[...] = d_pair[:earlier, :].astype(LOW)
    gains_ref[...] = jnp.zeros(gains_ref.shape, WIDE)
    gains_ref[0:1, :] = after_grad
    gains_ref[1:2, :] = feed_grad
    gains_ref[2:3, :] = final_grad
    gains_ref[3:4, :width] = query_grad
    wait_all(sent)


def closing_kernel(
    count, grad_count, table,
    own_ref, arrived_ref, x_ref, before_ref, key_gain_ref, cos_ref, sin_ref, d_normed_ref,
    d_hidden_ref, *refs,
):
    pieces = refs[:count]
    refs = refs[count:]
    grads = refs[:grad_count]
    input_ref, gains_ref, weights, grad_pair, sems, *out_sems = refs[grad_count:]
    width_pair = own_ref.shape[1]
    main = grads[0].shape[1] * len(grads)
    quarter = width_pair // HEADS
    half = width_pair // 2
    copies, sent = [], []
    for t in range(HEADS):
        columns = quarter_columns(table, t, quarter)
        copies += fetches(
            table, pieces, t, (width_pair, quarter), lambda rows: weights.at[rows, columns], sems
        )
    x = x_ref[...].astype(WIDE)
    normed = norm_rows(x, before_ref[...]).astype(LOW)
    d_pair = own_ref[...]
    for back in range(arrived_ref.shape[0]):
        d_pair = d_pair + arrived_ref[back].astype(WIDE)
    wait_all(copies)
    raw = dot(normed, weights[:, :half])
    d_key, key_grad = norm_back(
        raw, key_gain_ref[...], rotate(d_pair[:, :half], cos_ref[...], -sin_ref[...])
    )
    low_pair = jnp.concatenate([d_key.astype(LOW), d_pair[:, half:].astype(LOW)], axis=1)
    grad_pair[...] = dot_tn(normed, low_pair).astype(LOW)
    for t in range(HEADS):
        columns = quarter_columns(table, t, quarter)
        sent += sendings(
            table, len(pieces) + main, grads, t, lambda at: grad_pair.at[at, columns],
            (0, quarter), out_sems[t],
        )
    d_normed = d_normed_ref[...] + dot_nt(low_pair, weights[...])
    part_inputs, before_grad = norm_back(x, before_ref[...], d_normed)
    input_ref[...] = d_hidden_ref[...] + part_inputs
    gains_ref[...] = jnp.zeros(gains_ref.shape, WIDE)
    gains_ref[0:1, :] = before_grad
    gains_ref[1:2, :half] = key_grad
    wait_all(sent)


def call(kernel, name, args, far_args, outs, far_outs, scratch, sems, cost, aliases=None):
    anywhere = pl.BlockSpec(memory_space=pl.ANY)
    near = pl.BlockSpec(memory_space=pltpu.VMEM)
    flops, moved = cost
    return pl.pallas_call(
        kernel,
        name=name,
        out_shape=[jax.ShapeDtypeStruct(shape, dtype) for shape, dtype in far_outs + outs],
        in_specs=[pl.BlockSpec(memory_space=pltpu.SMEM)]
        + [near] * (len(args) - 1)
        + [anywhere] * len(far_args),
        out_specs=[anywhere] * len(far_outs) + [near] * len(outs),
        scratch_shapes=[pltpu.VMEM(shape, dtype) for shape, dtype in scratch]
        + [pltpu.SemaphoreType.DMA((count,)) for count in sems],
        input_output_aliases=aliases or {},
        cost_estimate=pl.CostEstimate(flops=flops, transcendentals=0, bytes_accessed=moved),
        compiler_params=pltpu.CompilerParams(vmem_limit_bytes=VMEM_BYTES),
    )(*args, *far_args)


def layer_keys(x, layer, turns, table):
    pieces, before, query_gain, key_gain, after_gain, feed_gain, final = layer
    far = tuple(pieces)
    pair = 2 * key_gain.shape[1]
    rows, width = x.shape
    args = (table, x, before, key_gain) + turns
    kernel = functools.partial(keys_kernel, len(far))
    cost = (2 * rows * width * pair, 2 * width * pair)
    outs = [((rows, pair), LOW)]
    return call(kernel, "keys", args, far, outs, [], [((width, pair), LOW)], [HEADS * len(far)], cost)[0]


def sizes_of(pieces, own):
    columns = pieces[0].shape[2]
    rest = columns - own - own // HEADS - EXTRA
    return columns, rest


def layer_forward(x, pair, layer, bias, turns, table):
    pieces, before, query_gain, key_gain, after_gain, feed_gain, final = layer
    far = tuple(pieces)
    rows, width = x.shape
    own = pair.shape[1]
    columns, rest = sizes_of(pieces, own)
    args = (table, x, pair, bias) + turns + (before, query_gain, after_gain, feed_gain, final)
    token = ((rows, width), WIDE)
    outs = [((rows, width), LOW), ((rows, own // 2 * HEADS), LOW), token, token, token]
    scratch = [((HEADS, width, own), LOW), ((HEADS, width, rest), LOW)]
    kernel = functools.partial(forward_kernel, len(far))
    cost = (4 * rows * width * columns * HEADS, 2 * width * columns * HEADS)
    return call(kernel, "forward", args, far, outs, [], scratch, [HEADS * len(far)] * 2, cost)


def layer_backward(dy, x, pair, kept, layer, bias, turns, table, ranks):
    pieces, before, query_gain, key_gain, after_gain, feed_gain, final = layer
    far = tuple(pieces)
    rows, width = x.shape
    own = pair.shape[1]
    columns, rest = sizes_of(pieces, own)
    earlier = pair.shape[0] - rows
    args = (
        (table, dy, x, pair, bias) + turns + (before, query_gain, after_gain, feed_gain, final)
        + tuple(kept)
    )
    token = ((rows, width), WIDE)
    if ranks > 4:
        grad_shapes = [((HEADS, 1, width, own + rest), LOW)]
        pair_shapes = [((HEADS, 1, width, own // HEADS), LOW)]
    else:
        half = width // (ranks * CORES)
        grad_shapes = [
            ((HEADS, len(group), half, own + rest), LOW)
            for group in groups_of(ranks)
            for core in range(CORES)
        ]
        pair_shapes = [((HEADS, ranks, half, own // HEADS), LOW)] * CORES
    count = sum(shape[1] for shape, dtype in grad_shapes)
    outs = [((rows, own), WIDE), ((earlier, own), LOW), token, token, ((8, width), WIDE)]
    scratch = [
        ((HEADS, width, own), LOW), ((HEADS, width, rest), LOW),
        ((HEADS, width, own), LOW), ((HEADS, width, rest), LOW), (pair.shape, WIDE),
    ]
    kernel = functools.partial(backward_kernel, len(far), len(grad_shapes))
    cost = (8 * rows * width * columns * HEADS, 4 * width * columns * HEADS)
    result = call(
        kernel, "backward", args, far, outs, grad_shapes, scratch,
        [HEADS * len(far)] * 2 + [count] * 2 * HEADS, cost,
    )
    grads = tuple(result[: len(grad_shapes)])
    d_own, sent, d_normed, d_hidden, gains = result[len(grad_shapes) :]
    back = earlier // rows
    arrived = jnp.stack(
        [
            shifted(sent[(back - by) * rows : (back - by + 1) * rows], HEAD, -by)
            for by in range(1, back + 1)
        ]
    )
    args = (table, d_own, arrived, x, before, key_gain) + turns + (d_normed, d_hidden)
    outs = [token, ((8, width), WIDE)]
    scratch = [((width, own), LOW), ((width, own), LOW)]
    kernel = functools.partial(closing_kernel, len(far), len(pair_shapes))
    cost = (6 * rows * width * own, 4 * width * own)
    result = call(
        kernel, "closing", args, far, outs, pair_shapes, scratch,
        [HEADS * len(far)] + [count] * HEADS, cost,
    )
    input_grad, more = result[len(pair_shapes) :]
    gain_grads = (
        more[0], gains[3, : own // 2], more[1, : own // 2], gains[0], gains[1], gains[2],
    )
    pairs = tuple(result[: len(pair_shapes)])
    gain_grads = jnp.concatenate([gain.reshape(ranks, -1) for gain in gain_grads], axis=1)
    if ranks <= 4:
        pairs = gains_beside(pairs, gain_grads, ranks)
    return input_grad, grads + pairs, gain_grads


def body(
    inputs,
    out_grad,
    segment_ids,
    positions,
    before_gain,
    query_matrix,
    key_matrix,
    value_matrix,
    query_gain,
    key_gain,
    output_matrix,
    after_gain,
    feed_gain,
    gate_matrix,
    up_matrix,
    down_matrix,
    final_gain,
):
    section = lax.axis_index(SECTION)
    head = lax.axis_index(HEAD)
    ranks = lax.axis_size(DATA)
    rows, width = inputs.shape[1:]
    head_width = key_matrix.shape[2]
    depth = gate_matrix.shape[1]
    hidden_width = gate_matrix.shape[2]
    back = min(-(-(WINDOW - 1) // rows), HEADS - 1)
    quarter = 2 * head_width // HEADS

    gain_list = (before_gain, query_gain, key_gain, after_gain, feed_gain, final_gain)
    sizes = [gain.shape[1] for gain in gain_list]
    gain_flat = jnp.concatenate([gain[0] for gain in gain_list])
    gain_block = jnp.zeros((depth, EXTRA), LOW)
    if ranks > 4:
        gain_both = gather_gains(gain_flat)
    else:
        lines = gain_flat.reshape(-1, EXTRA)
        for first in (0, depth // CORES):
            gain_block = lax.dynamic_update_slice(gain_block, lines, (first, 0))

    shared = jnp.concatenate([key_matrix[0], value_matrix[0]], axis=1)
    slab = jnp.concatenate(
        [
            query_matrix[0],
            output_matrix[0].T,
            lax.dynamic_slice_in_dim(shared, head * quarter, quarter, 1),
            gain_block,
            gate_matrix[0],
            up_matrix[0],
            down_matrix[0].T,
        ],
        axis=1,
    )
    half = depth // CORES
    upper, lower = slab[:half], slab[half:]
    traded = flip(jnp.where(section == 0, lower, upper), SECTION, 1)
    halves = jnp.where(section == 0, upper, traded), jnp.where(section == 0, traded, lower)

    first_pieces, chunks = gather_slab(halves[0])
    second_pieces, unused = gather_slab(after(halves[1], chunks[3]))
    pieces = first_pieces, second_pieces
    if ranks <= 4:
        gain_both = [gains_in(held, sum(sizes), 2 * head_width + quarter) for held in pieces]

    first_input = lax.dynamic_index_in_dim(inputs, section, 0, keepdims=False)
    last_cot = lax.dynamic_index_in_dim(out_grad, section, 0, keepdims=False)
    segments = lax.dynamic_index_in_dim(segment_ids, section, 0, keepdims=False)
    token_positions = lax.dynamic_index_in_dim(positions, section, 0, keepdims=False)
    everyone = jnp.concatenate(
        [shifted(after(first_input, chunks[1]), HEAD, by) for by in range(back, 0, -1)] + [first_input]
    )
    padded_segments = jnp.concatenate([jnp.full((back * rows,), -1, jnp.int32), segments])
    padded_positions = jnp.concatenate([jnp.zeros((back * rows,), jnp.int32), token_positions])
    key_segments = lax.dynamic_slice_in_dim(padded_segments, head * rows, (back + 1) * rows)
    key_positions = lax.dynamic_slice_in_dim(padded_positions, head * rows, (back + 1) * rows)
    gap = key_positions[-rows:, None] - key_positions[None, :]
    allowed = (
        (key_segments[-rows:, None] == key_segments[None, :]) & (gap >= 0) & (gap < WINDOW)
    )
    bias = jnp.where(allowed, 0.0, -1e30).astype(WIDE)
    half_depth = head_width // 2
    frequency = 10000.0 ** (-(jnp.arange(half_depth, dtype=WIDE) * 2.0) / head_width)
    turn = key_positions.astype(WIDE)[:, None] * frequency
    turns_all = jnp.cos(turn), jnp.sin(turn)
    turns = turns_all[0][-rows:], turns_all[1][-rows:]

    layers = []
    for index in range(2):
        gains, first = [], 0
        for size in sizes:
            gains.append(gain_both[index][:, first : first + size].reshape(1, -1).astype(WIDE))
            first += size
        layers.append((pieces[index],) + tuple(gains))

    table = row_table(ranks, depth)
    pair_first = layer_keys(everyone, layers[0], turns_all, table)
    out_first, *kept_first = layer_forward(first_input, pair_first, layers[0], bias, turns, table)
    own_pair = layer_keys(out_first, layers[1], turns, table)
    pair_second = jnp.concatenate(
        [shifted(own_pair, HEAD, by) for by in range(back, 0, -1)] + [own_pair]
    )
    out_second, *kept_second = layer_forward(
        out_first, pair_second, layers[1], bias, turns, table
    )
    grad_second, slab_second, gains_second = layer_backward(
        last_cot, out_first, pair_second, kept_second, layers[1], bias, turns, table, ranks
    )
    sums_second = first_sums(slab_second, ranks)
    grad_first, slab_first, gains_first = layer_backward(
        after(grad_second.astype(LOW), *sums_second), first_input, pair_first, kept_first, layers[0], bias, turns, table, ranks
    )
    total_second, unused = scatter_sums(sums_second, ranks)
    total_first, unused = scatter_sums(first_sums(slab_first, ranks), ranks)

    def settle(first, second):
        own, sent = by_section(first, second)
        return jnp.stack(by_section(own, flip(sent, SECTION, 1)))[None]

    own, sent = by_section(total_first, total_second)
    gain_own = (
        scatter_gains(gains_first, gains_second)
        if ranks > 4
        else own[: sum(sizes) // 128, slab.shape[1] - EXTRA :].reshape(-1)
    )
    gain_grads, first = [], 0
    for size in sizes:
        gain_grads.append(gain_own[None, first : first + size])
        first += size

    own = jnp.concatenate(by_section(own, flip(sent, SECTION, 1)))
    starts = [0]
    for step in (head_width, head_width, hidden_width, hidden_width, hidden_width, quarter):
        starts.append(starts[-1] + step)
    cut = [own[:, a:b] for a, b in zip(starts[:-1], starts[1:])]
    pair = cut[5].astype(LOW)
    shared = jnp.zeros((depth, 2 * head_width), LOW)
    for bit in range(HEADS):
        piece = pair if bit == 0 else flip(pair, HEAD, bit)
        shared = lax.dynamic_update_slice(shared, piece, (0, (head ^ bit) * quarter))
    shared = shared.astype(WIDE)
    return (
        settle(out_first, out_second),
        settle(grad_first, grad_second),
        gain_grads[0],
        cut[0][None],
        shared[None, :, :head_width],
        shared[None, :, head_width:],
        gain_grads[1],
        gain_grads[2],
        cut[1].T[None],
        gain_grads[3],
        gain_grads[4],
        cut[2][None],
        cut[3][None],
        cut[4].T[None],
        gain_grads[5],
    )


def solution(mesh):
    tokens = P(None, (DATA, HEAD), None)
    pack = P(None, DATA)
    gain = P(SECTION, DATA)
    split = P(SECTION, DATA, HEAD)
    plain = P(SECTION, DATA, None)
    turned = P(SECTION, HEAD, DATA)
    outs = P(SECTION, None, (DATA, HEAD), None)
    weights = (
        gain, split, plain, plain, gain, gain, turned, gain, gain, split, split, turned, gain,
    )
    return jax.shard_map(
        body,
        mesh=mesh,
        in_specs=(tokens, tokens, pack, pack) + weights,
        out_specs=(outs, outs) + weights,
        check_vma=False,
    )
```
